512 devices in a mesh: dp: 64 (over z, y_lo, core), tensor: 8 (over y_hi, x).
Axes of the slice: x: 4, y: 8 (y_hi: 2, y_lo: 4; y = y_hi * 4 + y_lo), z: 8, core: 2. Of those that a mesh axis runs over, the one named last changes fastest.
Arguments:
- tokens: bfloat16 [24576, 8192], P(('dp', 'tensor')), may hold values from -6 to 6
- grad_gate: bfloat16 [24576, 28672], P('dp', 'tensor'), may hold values from -1.25 to 1.25
- basis: bfloat16 [8192, 256], P(('dp', 'tensor')), may hold values from -0.375 to 0.375
- first_moment: float32 [256, 28672], P('dp', 'tensor'), may hold values from -0.375 to 0.375
- second_moment: float32 [256, 28672], P('dp', 'tensor'), may hold values from 0.02 to 0.2
Outputs:
- update: bfloat16 [8192, 28672], P('dp', 'tensor')
- first_out: float32 [256, 28672], P('dp', 'tensor')
- second_out: float32 [256, 28672], P('dp', 'tensor')
The draws below stay inside these ranges and needn't reach their ends.
All inputs are finite; a program needn't handle non-finite values.
Results may differ from the reference program's by a relative error of at most 0.0057.
Values may be sent and summed in bfloat16 or wider, within the bound.
No kernel may reach another device: no remote copies, remote signals or barrier semaphores. Data moves between devices by JAX's collectives and lax.ppermute only.
A program may use at most 64 MiB of HBM per device.

```python
import math
import jax
import jax.numpy as jnp

D = 8192
FF = 28672
R = 256
STEP = 10
TOKENS = 24576


def level_of(own_key, shape, split, low, largest):
    level, own = 1.0, jax.random.fold_in(own_key, 6)
    for position, shards_of in split:
        heights = jnp.exp(jax.random.uniform(jax.random.fold_in(own, position), (shards_of,), jnp.float32, low / len(split), largest / len(split)))
        level = level * jnp.repeat(heights, shape[position] // shards_of).reshape([-1 if axis == position else 1 for axis in range(len(shape))])
    return level


def bell_draw(rng, shape, width, bound, shards=(), held_as=jnp.bfloat16):
    result = width * jax.random.normal(rng, shape, jnp.float32)
    if shards:
        result = result * level_of(rng, shape, shards, -0.22, 0.18)
    return jnp.clip(result, -bound, bound).astype(held_as)


def setup_inputs(seed: int = 0) -> dict:
    key_of = jax.random.split(jax.random.key(seed), 6)
    return {
        "tokens": bell_draw(key_of[0], (TOKENS, D), 1.0, 6.0, ((0, 512),)),
        "grad_gate": bell_draw(key_of[1], (TOKENS, FF), 0.2, 1.25, ((0, 64), (1, 8))),
        "basis": bell_draw(key_of[2], (D, R), R ** -0.5, 0.375, ((0, 512),)),
        "first_moment": bell_draw(key_of[3], (R, FF), 0.06, 0.375, ((0, 64), (1, 8)), jnp.float32),
        "second_moment": jnp.clip(jnp.exp(math.log(0.2) - 2.3025851 * jax.random.uniform(key_of[4], (R, FF), jnp.float32) ** level_of(key_of[4], (R, FF), ((0, 64), (1, 8)), -0.2, 0.2)), 0.02, 0.2),
    }


BETA_ONE = 0.9
BETA_TWO = 0.95
EPS = 1e-08

def reference(tokens, grad_gate, basis, first_moment, second_moment):
    coefficients = jnp.dot(basis.T, tokens.T, preferred_element_type=jnp.float32).astype(jnp.bfloat16)
    inverse_root = 1.0 / math.sqrt(TOKENS)
    grad = jnp.dot(coefficients, grad_gate, preferred_element_type=jnp.float32) * inverse_root
    first_out = BETA_ONE * first_moment + (1.0 - BETA_ONE) * grad
    second_out = BETA_TWO * second_moment + (1.0 - BETA_TWO) * grad * grad
    corrected = first_out / (1.0 - BETA_ONE ** STEP)
    scaled = jnp.sqrt(second_out / (1.0 - BETA_TWO ** STEP)) + EPS
    direction = (corrected / scaled).astype(jnp.bfloat16)
    update = jnp.dot(basis, direction, preferred_element_type=jnp.float32).astype(jnp.bfloat16)
    return (update, first_out, second_out)
```

```python
import functools
import math

import jax
import jax.numpy as jnp
from jax import lax
from jax.experimental import pallas as pl
from jax.experimental.pallas import tpu as pltpu
from jax.sharding import Mesh
from jax.sharding import PartitionSpec as P

STEP = 10


BETA_ONE = 0.9
BETA_TWO = 0.95
EPS = 1e-08

Z, Y_LO, CORE, Y_HI, X = 8, 4, 2, 2, 4
CLASSES = CORE * X
OWNERS = Z * Y_LO
VMEM_LIMIT = 24 * 1024 * 1024
F32, BF16 = jnp.float32, jnp.bfloat16


def call(body, out_shape, flops, moved):
    return pl.pallas_call(
        body,
        out_shape=out_shape,
        compiler_params=pltpu.CompilerParams(vmem_limit_bytes=VMEM_LIMIT),
        cost_estimate=pl.CostEstimate(flops=flops, bytes_accessed=moved, transcendentals=0),
    )


def iota(shape, axis):
    return lax.broadcasted_iota(jnp.int32, shape, axis)


def one_hot(condition):
    return jnp.where(condition, 1.0, 0.0).astype(BF16)


def split_features(tokens_ref, out_ref):
    rows = tokens_ref.shape[0]
    width = Y_LO * 128
    p, q = iota((width, width), 0), iota((width, width), 1)
    place = ((p >> 4) & 3) * 128 + (p >> 7) * 32 + ((p >> 6) & 1) * 16 + (p & 15)
    move = one_hot(place == q)
    for z in range(Z):
        for core in range(CORE):
            block = jnp.concatenate(
                [
                    tokens_ref[:, pl.ds(((z * Y_LO + y) * CORE + core) * 128, 128)]
                    for y in range(Y_LO)
                ],
                axis=1,
            )
            moved = jnp.dot(block, move, preferred_element_type=F32).astype(BF16)
            for x in range(X):
                out_ref[pl.ds((core * X + x) * rows, rows), pl.ds(z * 128, 128)] = moved[
                    :, x * 128 : (x + 1) * 128
                ]


def partial_coefficients(tokens_ref, basis_ref, out_ref):
    out_ref[...] = jnp.dot(
        tokens_ref[...], basis_ref[...], preferred_element_type=F32
    ).astype(BF16)


def sum_coefficients(parts_ref, basis_ref, out_ref):
    rows = parts_ref.shape[0] // CLASSES
    own = basis_ref.shape[0]
    total = parts_ref[0:rows, :].astype(F32)
    for part in range(1, CLASSES):
        total += parts_ref[part * rows : (part + 1) * rows, :].astype(F32)
    total = total.astype(BF16)
    basis = basis_ref[...]
    count = out_ref.shape[0] // (rows + own)
    for copy in range(count):
        start = copy * (rows + own)
        out_ref[start : start + rows, :] = total
        out_ref[start + rows : start + rows + own, :] = basis


def rank_of(row, core):
    return (row >> 3) * 8 + core * 4 + (row & 3)


def project(scale, core_ref, gathered_ref, grad_ref, out_ref):
    core = core_ref[0]
    width = out_ref.shape[1]
    chunk = gathered_ref.shape[0] // 8
    tokens = chunk - 16
    coefficients = jnp.concatenate(
        [gathered_ref[t * chunk : t * chunk + tokens, :] for t in range(8)], axis=0
    )
    rank = coefficients.shape[1]
    rows = out_ref.shape[0]
    place = one_hot(rank_of(iota((rows, rank), 0), core) == iota((rows, rank), 1))
    arranged = lax.dot_general(
        place, coefficients, (((1,), (1,)), ((), ())), preferred_element_type=F32
    ).astype(BF16)
    tile = 256
    first_half = (iota((rows, tile), 0) & 4) == 0
    for start in range(0, width, tile):
        low = jnp.dot(
            arranged, grad_ref[:, start : start + tile], preferred_element_type=F32
        )
        high = jnp.dot(
            arranged,
            grad_ref[:, width + start : width + start + tile],
            preferred_element_type=F32,
        )
        out_ref[:, start : start + tile] = (
            jnp.where(first_half, low, high) * scale
        ).astype(out_ref.dtype)


def add_halves(mine_ref, theirs_ref, out_ref):
    out_ref[...] = (mine_ref[...] + theirs_ref[...].astype(F32)).astype(BF16)


def adam(parts_ref, first_ref, second_ref, first_out_ref, second_out_ref, out_ref):
    rows, width = 4, parts_ref.shape[1]
    total = parts_ref[0:16, :].astype(F32)
    for part in range(1, parts_ref.shape[0] // 16):
        total += parts_ref[part * 16 : (part + 1) * 16, :].astype(F32)
    total = total[0:8, :] + total[8:16, :]
    directions = []
    for half in range(2):
        grad = total[half * rows : (half + 1) * rows, :]
        columns = slice(half * width, (half + 1) * width)
        first_out = BETA_ONE * first_ref[:, columns] + (1.0 - BETA_ONE) * grad
        second_out = BETA_TWO * second_ref[:, columns] + (1.0 - BETA_TWO) * grad * grad
        first_out_ref[:, columns] = first_out
        second_out_ref[:, columns] = second_out
        corrected = first_out / (1.0 - BETA_ONE**STEP)
        scaled = jnp.sqrt(second_out / (1.0 - BETA_TWO**STEP)) + EPS
        directions.append(corrected / scaled)
    block = jnp.concatenate(directions + directions, axis=0).astype(BF16)
    for part in range(out_ref.shape[0] // 16):
        out_ref[part * 16 : (part + 1) * 16, :] = block


def expand(core_ref, gathered_ref, mine_ref, theirs_ref, out_ref):
    core = core_ref[0]
    chunk = gathered_ref.shape[0] // 8
    basis = jnp.concatenate(
        [gathered_ref[t * chunk + chunk - 16 : (t + 1) * chunk, :] for t in range(8)], axis=0
    )
    rank = basis.shape[1]
    width = mine_ref.shape[1]
    r, place = iota((rank, rank), 0), iota((rank, rank), 1)
    for half in range(2):
        in_half = ((place >> 2) & 1) == half
        own = one_hot((r == rank_of(place, core)) & in_half)
        other = one_hot((r == rank_of(place, 1 - core)) & in_half)
        own_basis = jnp.dot(basis, own, preferred_element_type=F32).astype(BF16)
        other_basis = jnp.dot(basis, other, preferred_element_type=F32).astype(BF16)
        tile = 256
        for start in range(0, width, tile):
            out_ref[:, half * width + start : half * width + start + tile] = (
                jnp.dot(
                    own_basis, mine_ref[:, start : start + tile], preferred_element_type=F32
                )
                + jnp.dot(
                    other_basis, theirs_ref[:, start : start + tile], preferred_element_type=F32
                )
            ).astype(BF16)


def per_device(tokens, grad_gate, basis, first_moment, second_moment):
    rows, features = tokens.shape
    own, rank = basis.shape
    group_tokens, columns = grad_gate.shape
    half_columns = columns // 2
    scale = 1.0 / math.sqrt(group_tokens * Z * Y_LO * CORE)
    shape = jax.ShapeDtypeStruct
    core = lax.axis_index("core").astype(jnp.int32)
    core_index = core.reshape(1)
    swap = [(0, 1), (1, 0)]

    basis_axes, class_axes, owner_axes = ("z", "y_lo", "y_hi"), ("core", "x"), ("z", "y_lo")
    tensor_axes = ("y_hi", "x")

    def exchange(array, axes):
        return lax.all_to_all(array, axes, 0, 0, tiled=True)

    copies = Z * Y_LO * Y_HI
    class_basis = exchange(
        jnp.broadcast_to(basis[None], (copies, own, rank)).reshape(copies * own, rank), basis_axes
    )
    split = call(
        split_features,
        shape((CLASSES * rows, features // CLASSES), BF16),
        2 * rows * features * 512,
        4 * rows * features,
    )(tokens)
    class_tokens = exchange(split, class_axes)
    parts = call(
        partial_coefficients,
        shape((CLASSES * rows, rank), BF16),
        2 * rows * features * rank,
        2 * (rows * features + copies * own * rank),
    )(class_tokens, class_basis)
    parts = exchange(parts, class_axes)
    chunk = rows + own
    summed = call(
        sum_coefficients,
        shape((8 * chunk, rank), BF16),
        CLASSES * rows * rank,
        4 * 8 * chunk * rank,
    )(parts, basis)
    gathered = exchange(summed, tensor_axes)

    smem = pl.BlockSpec(memory_space=pltpu.SMEM)
    vmem = pl.BlockSpec(memory_space=pltpu.VMEM)

    def projected(which, dtype):
        return pl.pallas_call(
            functools.partial(project, scale),
            out_shape=shape((rank, half_columns), dtype),
            in_specs=[smem, vmem, vmem],
            out_specs=vmem,
            compiler_params=pltpu.CompilerParams(vmem_limit_bytes=VMEM_LIMIT),
            cost_estimate=pl.CostEstimate(
                flops=2 * rank * group_tokens * columns,
                bytes_accessed=2 * group_tokens * columns + 2 * rank * columns,
                transcendentals=0,
            ),
        )(which, gathered, grad_gate)

    theirs = lax.ppermute(projected(1 - core_index, BF16), "core", swap)
    mine = projected(core_index, F32)
    pair = call(
        add_halves, shape((rank, half_columns), BF16), rank * half_columns, 8 * rank * half_columns
    )(mine, theirs)
    owned = exchange(pair, owner_axes)
    first_out, second_out, direction = call(
        adam,
        (
            shape(first_moment.shape, F32),
            shape(second_moment.shape, F32),
            shape((rank, half_columns), BF16),
        ),
        rank * half_columns,
        4 * rank * half_columns,
    )(owned, first_moment, second_moment)
    directions = exchange(direction, owner_axes)
    others = lax.ppermute(directions, "core", swap)
    update = pl.pallas_call(
        expand,
        out_shape=shape((own * 8, columns), BF16),
        in_specs=[smem, vmem, vmem, vmem],
        out_specs=vmem,
        compiler_params=pltpu.CompilerParams(vmem_limit_bytes=VMEM_LIMIT),
        cost_estimate=pl.CostEstimate(
            flops=4 * own * 8 * rank * columns,
            bytes_accessed=4 * rank * columns,
            transcendentals=0,
        ),
    )(core_index, gathered, directions, others)
    return (update, first_out, second_out)


def solution(mesh):
    names = ("z", "y_lo", "core", "y_hi", "x")
    fine = Mesh(mesh.devices.reshape(Z, Y_LO, CORE, Y_HI, X), names)
    data, tensor = names[:3], names[3:]
    placed = (P(names, None), P(data, tensor), P(names, None), P(data, tensor), P(data, tensor))
    return jax.shard_map(
        per_device,
        mesh=fine,
        in_specs=placed,
        out_specs=(P(data, tensor), P(data, tensor), P(data, tensor)),
        check_vma=False,
    )
```

```python
import functools
import math

import jax
import jax.numpy as jnp
from jax import lax
from jax.experimental import pallas as pl
from jax.experimental.pallas import tpu as pltpu
from jax.sharding import Mesh
from jax.sharding import PartitionSpec as P

STEP = 10


BETA_ONE = 0.9
BETA_TWO = 0.95
EPS = 1e-08

Z, Y_LO, CORE, Y_HI, X = 8, 4, 2, 2, 4
CLASSES = CORE * X
OWNERS = Z * Y_LO
SPLIT_FLOPS = 2 * 48 * 8192 * 512
VMEM_LIMIT = 24 * 1024 * 1024
F32, BF16 = jnp.float32, jnp.bfloat16


def call(body, out_shape, flops, moved, placed=False):
    vmem = pl.BlockSpec(memory_space=pltpu.VMEM)
    smem = pl.BlockSpec(memory_space=pltpu.SMEM)

    def run(*operands):
        specs = [smem if placed and n == 0 else vmem for n in range(len(operands))]
        return pl.pallas_call(
            body,
            out_shape=out_shape,
            in_specs=specs,
            out_specs=jax.tree.map(lambda _: vmem, out_shape),
            compiler_params=pltpu.CompilerParams(vmem_limit_bytes=VMEM_LIMIT),
            cost_estimate=pl.CostEstimate(flops=flops, bytes_accessed=moved, transcendentals=0),
        )(*operands)

    return run


def iota(shape, axis):
    return lax.broadcasted_iota(jnp.int32, shape, axis)


def one_hot(condition):
    return jnp.where(condition, 1.0, 0.0).astype(BF16)


def split_features(at_ref, tokens_ref, *out_refs):
    core, here = at_ref[0], at_ref[1]
    width = Y_LO * 128
    p, q = iota((width, width), 0), iota((width, width), 1)
    steps = (((p >> 4) & 3) - here) & 3
    move = one_hot(steps * 128 + (p >> 7) * 32 + ((p >> 6) & 1) * 16 + (p & 15) == q)
    for z in range(Z):
        for step in range(CORE):
            side = core if step == 0 else 1 - core
            block = jnp.concatenate(
                [
                    tokens_ref[
                        :,
                        pl.ds(pl.multiple_of((z * Y_LO + y) * CORE * 128 + side * 128, 128), 128),
                    ]
                    for y in range(Y_LO)
                ],
                axis=1,
            )
            moved = jnp.dot(block, move, preferred_element_type=F32).astype(BF16)
            for x in range(X):
                out_refs[x][step, :, z * 128 : (z + 1) * 128] = moved[:, x * 128 : (x + 1) * 128]


def partial_coefficients(at_ref, basis_ref, sibling_ref, *refs):
    *token_refs, out_ref = refs
    core, here = at_ref[0], at_ref[1]
    rows = sibling_ref.shape[1]
    tokens = jnp.concatenate(
        [ref[0] for ref in token_refs] + [sibling_ref[step] for step in range(X)], axis=0
    )
    parts = jnp.dot(tokens, basis_ref[...], preferred_element_type=F32).astype(out_ref.dtype)
    for source in range(CLASSES):
        side = core if source < X else 1 - core
        place = side * X + ((here - source) & 3)
        out_ref[place] = parts[source * rows : (source + 1) * rows, :]


def sum_coefficients(parts_ref, basis_ref, out_ref):
    rows = parts_ref.shape[1]
    own = basis_ref.shape[0]
    total = parts_ref[0].astype(F32)
    for part in range(1, CLASSES):
        total += parts_ref[part].astype(F32)
    total = total.astype(BF16)
    basis = basis_ref[...]
    for copy in range(out_ref.shape[0]):
        out_ref[copy, 0:rows, :] = total
        out_ref[copy, rows : rows + own, :] = basis


def project(scale, at_ref, gathered_ref, grad_ref, other_ref, out_ref):
    core = at_ref[0]
    rank, width = out_ref.shape
    rows = gathered_ref.shape[1] - 16
    eye = one_hot(iota((rank, rank), 0) == iota((rank, rank), 1))

    def coefficients(side):
        stacked = jnp.concatenate(
            [gathered_ref[side * 8 + t, 0:rows, :] for t in range(8)], axis=0
        )
        return lax.dot_general(
            eye, stacked, (((1,), (1,)), ((), ())), preferred_element_type=F32
        ).astype(BF16)

    own, other = coefficients(core), coefficients(1 - core)
    tile = 256
    for start in range(0, width, tile):
        columns = pl.ds(pl.multiple_of(core * width + start, 128), tile)
        total = jnp.dot(own, grad_ref[:, columns], preferred_element_type=F32) + jnp.dot(
            other, other_ref[:, start : start + tile], preferred_element_type=F32
        )
        out_ref[:, start : start + tile] = (total * scale).astype(BF16)


def adam(
    at_ref, parts_ref, moments_ref, other_ref, kept_ref, sent_ref, out_ref
):
    core = at_ref[0]
    rows = 4
    total = parts_ref[0:16, :].astype(F32)
    for part in range(1, parts_ref.shape[0] // 16):
        total += parts_ref[part * 16 : (part + 1) * 16, :].astype(F32)
    grad = total[0:8, :] + total[8:16, :]

    def both(own, other):
        return jnp.where(
            core == 0,
            jnp.concatenate([own, other], axis=0),
            jnp.concatenate([other, own], axis=0),
        )

    first = both(moments_ref[0:rows, :], other_ref[0:rows, :])
    second = both(moments_ref[rows : 2 * rows, :], other_ref[rows : 2 * rows, :])
    first_out = BETA_ONE * first + (1.0 - BETA_ONE) * grad
    second_out = BETA_TWO * second + (1.0 - BETA_TWO) * grad * grad
    corrected = first_out / (1.0 - BETA_ONE**STEP)
    scaled = jnp.sqrt(second_out / (1.0 - BETA_TWO**STEP)) + EPS
    direction = corrected / scaled
    low = jnp.concatenate([first_out[0:rows, :], second_out[0:rows, :]], axis=0)
    high = jnp.concatenate([first_out[rows:, :], second_out[rows:, :]], axis=0)
    kept_ref[...] = jnp.where(core == 0, low, high)
    sent_ref[...] = jnp.where(core == 0, high, low)
    block = jnp.concatenate([direction, direction], axis=0).astype(BF16)
    for part in range(out_ref.shape[0] // 16):
        out_ref[part * 16 : (part + 1) * 16, :] = block


def group_basis(gathered_ref, side):
    rows = gathered_ref.shape[1]
    return jnp.concatenate(
        [gathered_ref[side * 8 + t, rows - 16 : rows, :] for t in range(8)], axis=0
    )


def expand_sent(
    at_ref, gathered_ref, directions_ref, kept_ref, other_ref, out_ref, first_ref, second_ref
):
    core = at_ref[0]
    basis = group_basis(gathered_ref, 1 - core)
    width = out_ref.shape[1]
    tile = 256
    for start in range(0, width, tile):
        out_ref[:, start : start + tile] = jnp.dot(
            basis, directions_ref[:, start : start + tile], preferred_element_type=F32
        ).astype(BF16)
    mine = pl.ds(pl.multiple_of(core * width, 128), width)
    theirs = pl.ds(pl.multiple_of((1 - core) * width, 128), width)
    first_ref[:, mine] = kept_ref[0:4, :]
    first_ref[:, theirs] = other_ref[0:4, :]
    second_ref[:, mine] = kept_ref[4:8, :]
    second_ref[:, theirs] = other_ref[4:8, :]


def expand(at_ref, gathered_ref, directions_ref, received_ref, out_ref):
    core = at_ref[0]
    basis = group_basis(gathered_ref, core)
    width = received_ref.shape[1]
    tile = 256
    for start in range(0, width, tile):
        mine = pl.ds(pl.multiple_of(core * width + start, 128), tile)
        theirs = pl.ds(pl.multiple_of((1 - core) * width + start, 128), tile)
        out_ref[:, mine] = jnp.dot(
            basis, directions_ref[:, start : start + tile], preferred_element_type=F32
        ).astype(BF16)
        out_ref[:, theirs] = received_ref[:, start : start + tile]


def per_device(tokens, grad_gate, basis, first_moment, second_moment):
    rows, features = tokens.shape
    own, rank = basis.shape
    group_tokens, columns = grad_gate.shape
    half = columns // 2
    moment_rows = first_moment.shape[0]
    scale = 1.0 / math.sqrt(group_tokens * Z * Y_LO * CORE)
    shape = jax.ShapeDtypeStruct
    core = lax.axis_index("core").astype(jnp.int32)
    at = jnp.stack([core, lax.axis_index("x").astype(jnp.int32)])
    swap = [(0, 1), (1, 0)]

    def exchange(array, axes):
        return lax.all_to_all(array, axes, 0, 0, tiled=True)

    def half_of(array, side):
        return lax.dynamic_slice_in_dim(array, side * half, half, 1)

    copies = Z * Y_LO * Y_HI
    class_basis = exchange(
        jnp.broadcast_to(basis[None], (copies, own, rank)), ("z", "y_lo", "y_hi")
    ).reshape(copies * own, rank)

    block = shape((CORE, rows, features // CLASSES), BF16)
    blocks = call(split_features, (block,) * X, SPLIT_FLOPS, 0, True)(at, tokens)
    held = [blocks[0]] + [
        lax.ppermute(blocks[step], "x", [(x, (x + step) % X) for x in range(X)])
        for step in range(1, X)
    ]
    sibling = lax.ppermute(jnp.stack([each[1] for each in held]), "core", swap)
    other_grad = lax.ppermute(half_of(grad_gate, 1 - core), "core", swap)
    moments = jnp.concatenate([first_moment, second_moment], axis=0)
    other_moments = lax.ppermute(half_of(moments, 1 - core), "core", swap)
    own_moments = half_of(moments, core)

    parts = call(
        partial_coefficients,
        shape((CLASSES, rows, rank), BF16),
        2 * rows * features * rank,
        2 * (rows * features + copies * own * rank),
        True,
    )(at, class_basis, sibling, *held)
    parts = exchange(parts, ("core", "x"))
    takers = CORE * Y_HI * X
    summed = call(
        sum_coefficients,
        shape((takers, rows + own, rank), BF16),
        CLASSES * rows * rank,
        2 * takers * (rows + own) * rank,
    )(parts, basis)
    gathered = exchange(summed, ("core", "y_hi", "x"))
    pair = call(
        functools.partial(project, scale),
        shape((rank, half), BF16),
        2 * rank * group_tokens * columns,
        2 * group_tokens * columns,
        True,
    )(at, gathered, grad_gate, other_grad)
    owned = exchange(pair, ("z", "y_lo"))
    kept, sent, direction = call(
        adam,
        (
            shape((2 * moment_rows, half), F32),
            shape((2 * moment_rows, half), F32),
            shape((rank, half), BF16),
        ),
        rank * half,
        4 * rank * half,
        True,
    )(at, owned, own_moments, other_moments)
    directions = exchange(direction, ("z", "y_lo"))
    other = lax.ppermute(sent, "core", swap)
    update_rows = own * Y_HI * X
    to_send, first_out, second_out = call(
        expand_sent,
        (
            shape((update_rows, half), BF16),
            shape(first_moment.shape, F32),
            shape(second_moment.shape, F32),
        ),
        2 * update_rows * rank * half,
        2 * rank * half,
        True,
    )(at, gathered, directions, kept, other)
    received = lax.ppermute(to_send, "core", swap)
    update = call(
        expand,
        shape((update_rows, columns), BF16),
        2 * update_rows * rank * half,
        2 * rank * columns,
        True,
    )(at, gathered, directions, received)
    return (update, first_out, second_out)


def solution(mesh):
    names = ("z", "y_lo", "core", "y_hi", "x")
    fine = Mesh(mesh.devices.reshape(Z, Y_LO, CORE, Y_HI, X), names)
    data, tensor = names[:3], names[3:]
    placed = (P(names, None), P(data, tensor), P(names, None), P(data, tensor), P(data, tensor))
    return jax.shard_map(
        per_device,
        mesh=fine,
        in_specs=placed,
        out_specs=(P(data, tensor), P(data, tensor), P(data, tensor)),
        check_vma=False,
    )
```

```python
import functools
import math

import jax
import jax.numpy as jnp
from jax import lax
from jax.experimental import pallas as pl
from jax.experimental.pallas import tpu as pltpu
from jax.sharding import Mesh
from jax.sharding import PartitionSpec as P

STEP = 10


BETA_ONE = 0.9
BETA_TWO = 0.95
EPS = 1e-08

Z, Y_LO, CORE, Y_HI, X = 8, 4, 2, 2, 4
CLASSES = CORE * X
OWNERS = Z * Y_LO
VMEM_LIMIT = 24 * 1024 * 1024
F32, BF16 = jnp.float32, jnp.bfloat16


def call(body, out_shape, flops, moved, placed=False):
    vmem = pl.BlockSpec(memory_space=pltpu.VMEM)
    smem = pl.BlockSpec(memory_space=pltpu.SMEM)

    def run(*operands):
        specs = [smem if placed and n == 0 else vmem for n in range(len(operands))]
        return pl.pallas_call(
            body,
            out_shape=out_shape,
            in_specs=specs,
            out_specs=jax.tree.map(lambda _: vmem, out_shape),
            compiler_params=pltpu.CompilerParams(vmem_limit_bytes=VMEM_LIMIT),
            cost_estimate=pl.CostEstimate(flops=flops, bytes_accessed=moved, transcendentals=0),
        )(*operands)

    return run


def iota(shape, axis):
    return lax.broadcasted_iota(jnp.int32, shape, axis)


def one_hot(condition):
    return jnp.where(condition, 1.0, 0.0).astype(BF16)


def side_block(z, y_lo, side):
    return pl.ds(pl.multiple_of(((z * Y_LO + y_lo) * CORE + side) * 128, 128), 128)


def take_sibling(at_ref, tokens_ref, basis_ref, out_ref, copies_ref):
    side = 1 - at_ref[0]
    for z in range(Z):
        for y in range(Y_LO):
            out_ref[:, (z * Y_LO + y) * 128 : (z * Y_LO + y + 1) * 128] = tokens_ref[
                :, side_block(z, y, side)
            ]
    basis = basis_ref[...]
    for copy in range(copies_ref.shape[0]):
        copies_ref[copy] = basis


def split_features(at_ref, tokens_ref, sibling_ref, *out_refs):
    core, here = at_ref[0], at_ref[1]
    rows = tokens_ref.shape[0]
    width = Y_LO * 128
    p, q = iota((width, width), 0), iota((width, width), 1)
    steps = (((p >> 4) & 3) - here) & 3
    move = one_hot(steps * 128 + (p >> 7) * 32 + ((p >> 6) & 1) * 16 + (p & 15) == q)
    for z in range(Z):
        own = jnp.concatenate(
            [tokens_ref[:, side_block(z, y, core)] for y in range(Y_LO)], axis=1
        )
        other = sibling_ref[:, z * width : (z + 1) * width]
        moved = jnp.dot(
            jnp.concatenate([own, other], axis=0), move, preferred_element_type=F32
        ).astype(BF16)
        for x in range(X):
            out_refs[x][:, z * 128 : (z + 1) * 128] = moved[:, x * 128 : (x + 1) * 128]


def partial_coefficients(at_ref, basis_ref, *refs):
    *token_refs, out_ref = refs
    core, here = at_ref[0], at_ref[1]
    rows = out_ref.shape[1]
    tokens = jnp.concatenate([ref[...] for ref in token_refs], axis=0)
    parts = jnp.dot(tokens, basis_ref[...], preferred_element_type=F32)
    for step in range(X):
        x = (here - step) & 3
        for other in range(CORE):
            side = core if other == 0 else 1 - core
            start = (step * CORE + other) * rows
            out_ref[side * X + x] = parts[start : start + rows, :]


def sum_coefficients(parts_ref, basis_ref, out_ref):
    rows = parts_ref.shape[1]
    own = basis_ref.shape[0]
    total = parts_ref[0]
    for part in range(1, CLASSES):
        total += parts_ref[part]
    total = total.astype(BF16)
    basis = basis_ref[...]
    for copy in range(out_ref.shape[0]):
        out_ref[copy, 0:rows, :] = total
        out_ref[copy, rows : rows + own, :] = basis


def rank_of(row, core):
    return (row >> 3) * 8 + core * 4 + (row & 3)


def project(scale, core_ref, gathered_ref, grad_ref, out_ref):
    core = core_ref[0]
    width = out_ref.shape[1]
    chunk = gathered_ref.shape[0] // 8
    tokens = chunk - 16
    coefficients = jnp.concatenate(
        [gathered_ref[t * chunk : t * chunk + tokens, :] for t in range(8)], axis=0
    )
    rank = coefficients.shape[1]
    rows = out_ref.shape[0]
    place = one_hot(rank_of(iota((rows, rank), 0), core) == iota((rows, rank), 1))
    arranged = lax.dot_general(
        place, coefficients, (((1,), (1,)), ((), ())), preferred_element_type=F32
    ).astype(BF16)
    tile = 256
    first_half = (iota((rows, tile), 0) & 4) == 0
    for start in range(0, width, tile):
        low = jnp.dot(
            arranged, grad_ref[:, start : start + tile], preferred_element_type=F32
        )
        high = jnp.dot(
            arranged,
            grad_ref[:, width + start : width + start + tile],
            preferred_element_type=F32,
        )
        out_ref[:, start : start + tile] = (
            jnp.where(first_half, low, high) * scale
        ).astype(out_ref.dtype)


def add_halves(mine_ref, theirs_ref, out_ref):
    out_ref[...] = (mine_ref[...] + theirs_ref[...].astype(F32)).astype(BF16)


def adam(parts_ref, first_ref, second_ref, first_out_ref, second_out_ref, out_ref):
    rows, width = 4, parts_ref.shape[1]
    total = parts_ref[0:16, :].astype(F32)
    for part in range(1, parts_ref.shape[0] // 16):
        total += parts_ref[part * 16 : (part + 1) * 16, :].astype(F32)
    total = total[0:8, :] + total[8:16, :]
    directions = []
    for half in range(2):
        grad = total[half * rows : (half + 1) * rows, :]
        columns = slice(half * width, (half + 1) * width)
        first_out = BETA_ONE * first_ref[:, columns] + (1.0 - BETA_ONE) * grad
        second_out = BETA_TWO * second_ref[:, columns] + (1.0 - BETA_TWO) * grad * grad
        first_out_ref[:, columns] = first_out
        second_out_ref[:, columns] = second_out
        corrected = first_out / (1.0 - BETA_ONE**STEP)
        scaled = jnp.sqrt(second_out / (1.0 - BETA_TWO**STEP)) + EPS
        directions.append(corrected / scaled)
    block = jnp.concatenate(directions + directions, axis=0).astype(BF16)
    for part in range(out_ref.shape[0] // 16):
        out_ref[part * 16 : (part + 1) * 16, :] = block


def expand(core_ref, gathered_ref, mine_ref, theirs_ref, out_ref):
    core = core_ref[0]
    chunk = gathered_ref.shape[0] // 8
    basis = jnp.concatenate(
        [gathered_ref[t * chunk + chunk - 16 : (t + 1) * chunk, :] for t in range(8)], axis=0
    )
    rank = basis.shape[1]
    width = mine_ref.shape[1]
    r, place = iota((rank, rank), 0), iota((rank, rank), 1)
    for half in range(2):
        in_half = ((place >> 2) & 1) == half
        own = one_hot((r == rank_of(place, core)) & in_half)
        other = one_hot((r == rank_of(place, 1 - core)) & in_half)
        own_basis = jnp.dot(basis, own, preferred_element_type=F32).astype(BF16)
        other_basis = jnp.dot(basis, other, preferred_element_type=F32).astype(BF16)
        tile = 256
        for start in range(0, width, tile):
            out_ref[:, half * width + start : half * width + start + tile] = (
                jnp.dot(
                    own_basis, mine_ref[:, start : start + tile], preferred_element_type=F32
                )
                + jnp.dot(
                    other_basis, theirs_ref[:, start : start + tile], preferred_element_type=F32
                )
            ).astype(BF16)


def per_device(tokens, grad_gate, basis, first_moment, second_moment):
    rows, features = tokens.shape
    own, rank = basis.shape
    group_tokens, columns = grad_gate.shape
    half = columns // 2
    scale = 1.0 / math.sqrt(group_tokens * Z * Y_LO * CORE)
    shape = jax.ShapeDtypeStruct
    core = lax.axis_index("core").astype(jnp.int32)
    at = jnp.stack([core, lax.axis_index("x").astype(jnp.int32)])
    sibling_at = jnp.stack([1 - core, lax.axis_index("x").astype(jnp.int32)])
    swap = [(0, 1), (1, 0)]

    def exchange(array, axes):
        return lax.all_to_all(array, axes, 0, 0, tiled=True)

    copies = Z * Y_LO * Y_HI
    for_sibling, basis_copies = call(
        take_sibling,
        (shape((rows, features // CORE), BF16), shape((copies, own, rank), BF16)),
        0,
        2 * (rows * features + copies * own * rank),
        True,
    )(at, tokens, basis)
    sibling = lax.ppermute(for_sibling, "core", swap)
    class_basis = exchange(basis_copies, ("z", "y_lo", "y_hi")).reshape(copies * own, rank)
    block = shape((CORE * rows, features // CLASSES), BF16)
    blocks = call(split_features, (block,) * X, 2 * rows * features * 512, 0, True)(
        at, tokens, sibling
    )
    held = [blocks[0]] + [
        lax.ppermute(blocks[step], "x", [(x, (x + step) % X) for x in range(X)])
        for step in range(1, X)
    ]
    parts = call(
        partial_coefficients,
        shape((CLASSES, rows, rank), F32),
        2 * rows * features * rank,
        2 * (rows * features + copies * own * rank),
        True,
    )(at, class_basis, *held)
    parts = exchange(parts, ("core", "x"))
    takers = Y_HI * X
    chunk = rows + own
    gathered = exchange(
        call(
            sum_coefficients,
            shape((takers, chunk, rank), BF16),
            CLASSES * rows * rank,
            4 * takers * chunk * rank,
        )(parts, basis),
        ("y_hi", "x"),
    ).reshape(takers * chunk, rank)

    def projected(which, dtype):
        return call(
            functools.partial(project, scale),
            shape((rank, half), dtype),
            2 * rank * group_tokens * columns,
            2 * group_tokens * columns + 2 * rank * columns,
            True,
        )(which, gathered, grad_gate)

    theirs = lax.ppermute(projected(sibling_at, BF16), "core", swap)
    mine = projected(at, F32)
    pair = call(add_halves, shape((rank, half), BF16), rank * half, 8 * rank * half)(mine, theirs)
    owned = exchange(pair, ("z", "y_lo"))
    first_out, second_out, direction = call(
        adam,
        (
            shape(first_moment.shape, F32),
            shape(second_moment.shape, F32),
            shape((rank, half), BF16),
        ),
        rank * half,
        4 * rank * half,
    )(owned, first_moment, second_moment)
    directions = exchange(direction, ("z", "y_lo"))
    others = lax.ppermute(directions, "core", swap)
    update = call(
        expand,
        shape((own * takers, columns), BF16),
        4 * own * takers * rank * columns,
        4 * rank * columns,
        True,
    )(at, gathered, directions, others)
    return (update, first_out, second_out)


def solution(mesh):
    names = ("z", "y_lo", "core", "y_hi", "x")
    fine = Mesh(mesh.devices.reshape(Z, Y_LO, CORE, Y_HI, X), names)
    data, tensor = names[:3], names[3:]
    placed = (P(names, None), P(data, tensor), P(names, None), P(data, tensor), P(data, tensor))
    return jax.shard_map(
        per_device,
        mesh=fine,
        in_specs=placed,
        out_specs=(P(data, tensor), P(data, tensor), P(data, tensor)),
        check_vma=False,
    )
```

```python
import functools
import math

import jax
import jax.numpy as jnp
from jax import lax
from jax.experimental import pallas as pl
from jax.experimental.pallas import tpu as pltpu
from jax.sharding import Mesh
from jax.sharding import PartitionSpec as P

STEP = 10


BETA_ONE = 0.9
BETA_TWO = 0.95
EPS = 1e-08

Z, Y_LO, CORE, Y_HI, X = 8, 4, 2, 2, 4
CLASSES = CORE * X
OWNERS = Z * Y_LO
VMEM_LIMIT = 24 * 1024 * 1024
MOST_VMEM = 58 * 1024 * 1024
F32, BF16 = jnp.float32, jnp.bfloat16


def call(body, out_shape, flops, moved, places="", scratch=(), limit=VMEM_LIMIT):
    vmem = pl.BlockSpec(memory_space=pltpu.VMEM)
    spaces = {"s": pl.BlockSpec(memory_space=pltpu.SMEM), "h": pl.BlockSpec(memory_space=pl.ANY)}

    def run(*operands):
        where = places.ljust(len(operands), "v")
        return pl.pallas_call(
            body,
            out_shape=out_shape,
            in_specs=[spaces.get(place, vmem) for place in where],
            out_specs=jax.tree.map(lambda _: vmem, out_shape),
            scratch_shapes=scratch,
            compiler_params=pltpu.CompilerParams(vmem_limit_bytes=limit),
            cost_estimate=pl.CostEstimate(flops=flops, bytes_accessed=moved, transcendentals=0),
        )(*operands)

    return run


def iota(shape, axis):
    return lax.broadcasted_iota(jnp.int32, shape, axis)


def one_hot(condition):
    return jnp.where(condition, 1.0, 0.0).astype(BF16)


def side_block(z, y_lo, side):
    return pl.ds(pl.multiple_of(((z * Y_LO + y_lo) * CORE + side) * 128, 128), 128)


def take_side(side, tokens_ref, out_ref, sems):
    return [
        pltpu.make_async_copy(
            tokens_ref.at[:, side_block(n // Y_LO, n % Y_LO, side)],
            out_ref.at[:, n * 128 : (n + 1) * 128],
            sems.at[n],
        )
        for n in range(Z * Y_LO)
    ]


def take_sibling(at_ref, tokens_ref, out_ref, sems):
    copies = take_side(1 - at_ref[0], tokens_ref, out_ref, sems)
    for copy in copies:
        copy.start()
    for copy in copies:
        copy.wait()


def split_features(at_ref, tokens_ref, sibling_ref, *refs):
    *out_refs, own_ref, sems = refs
    core, here = at_ref[0], at_ref[1]
    copies = take_side(core, tokens_ref, own_ref, sems)
    for copy in copies:
        copy.start()
    width = Y_LO * 128
    p, q = iota((width, width), 0), iota((width, width), 1)
    steps = (((p >> 4) & 3) - here) & 3
    move = one_hot(steps * 128 + (p >> 7) * 32 + ((p >> 6) & 1) * 16 + (p & 15) == q)
    for copy in copies:
        copy.wait()
    for z in range(Z):
        columns = slice(z * width, (z + 1) * width)
        both = jnp.concatenate([own_ref[:, columns], sibling_ref[:, columns]], axis=0)
        moved = jnp.dot(both, move, preferred_element_type=F32).astype(BF16)
        for x in range(X):
            out_refs[x][:, z * 128 : (z + 1) * 128] = moved[:, x * 128 : (x + 1) * 128]


def partial_coefficients(at_ref, basis_ref, *refs):
    *token_refs, out_ref, held_ref, sems = refs
    core, here = at_ref[0], at_ref[1]
    rows = out_ref.shape[1]
    copies = [
        pltpu.make_async_copy(ref, held_ref.at[step], sems.at[step])
        for step, ref in enumerate(token_refs)
    ]
    for copy in copies:
        copy.start()
    for step in range(X):
        x = (here - step) & 3
        copies[step].wait()
        parts = jnp.dot(held_ref[step], basis_ref[...], preferred_element_type=F32)
        for other in range(CORE):
            side = core if other == 0 else 1 - core
            out_ref[side * X + x] = parts[other * rows : (other + 1) * rows, :]


def sum_coefficients(parts_ref, basis_ref, out_ref):
    rows = parts_ref.shape[1]
    own = basis_ref.shape[0]
    total = parts_ref[0]
    for part in range(1, CLASSES):
        total += parts_ref[part]
    total = total.astype(BF16)
    basis = basis_ref[...]
    for copy in range(out_ref.shape[0]):
        out_ref[copy, 0:rows, :] = total
        out_ref[copy, rows : rows + own, :] = basis


def rank_of(row, core):
    return (row >> 3) * 8 + core * 4 + (row & 3)


def project(scale, core_ref, gathered_ref, grad_ref, out_ref):
    core = core_ref[0]
    width = out_ref.shape[1]
    chunk = gathered_ref.shape[0] // 8
    tokens = chunk - 16
    coefficients = jnp.concatenate(
        [gathered_ref[t * chunk : t * chunk + tokens, :] for t in range(8)], axis=0
    )
    rank = coefficients.shape[1]
    rows = out_ref.shape[0]
    place = one_hot(rank_of(iota((rows, rank), 0), core) == iota((rows, rank), 1))
    arranged = lax.dot_general(
        place, coefficients, (((1,), (1,)), ((), ())), preferred_element_type=F32
    ).astype(BF16)
    tile = 256
    first_half = (iota((rows, tile), 0) & 4) == 0
    for start in range(0, width, tile):
        low = jnp.dot(
            arranged, grad_ref[:, start : start + tile], preferred_element_type=F32
        )
        high = jnp.dot(
            arranged,
            grad_ref[:, width + start : width + start + tile],
            preferred_element_type=F32,
        )
        out_ref[:, start : start + tile] = (
            jnp.where(first_half, low, high) * scale
        ).astype(out_ref.dtype)


def add_halves(mine_ref, theirs_ref, out_ref):
    out_ref[...] = (mine_ref[...] + theirs_ref[...].astype(F32)).astype(BF16)


def adam(parts_ref, first_ref, second_ref, first_out_ref, second_out_ref, out_ref):
    rows, width = 4, parts_ref.shape[1]
    total = parts_ref[0:16, :].astype(F32)
    for part in range(1, parts_ref.shape[0] // 16):
        total += parts_ref[part * 16 : (part + 1) * 16, :].astype(F32)
    total = total[0:8, :] + total[8:16, :]
    directions = []
    for half in range(2):
        grad = total[half * rows : (half + 1) * rows, :]
        columns = slice(half * width, (half + 1) * width)
        first_out = BETA_ONE * first_ref[:, columns] + (1.0 - BETA_ONE) * grad
        second_out = BETA_TWO * second_ref[:, columns] + (1.0 - BETA_TWO) * grad * grad
        first_out_ref[:, columns] = first_out
        second_out_ref[:, columns] = second_out
        corrected = first_out / (1.0 - BETA_ONE**STEP)
        scaled = jnp.sqrt(second_out / (1.0 - BETA_TWO**STEP)) + EPS
        directions.append(corrected / scaled)
    block = jnp.concatenate(directions + directions, axis=0).astype(BF16)
    for part in range(out_ref.shape[0] // 16):
        out_ref[part * 16 : (part + 1) * 16, :] = block


def expand(core_ref, gathered_ref, mine_ref, theirs_ref, out_ref):
    core = core_ref[0]
    chunk = gathered_ref.shape[0] // 8
    basis = jnp.concatenate(
        [gathered_ref[t * chunk + chunk - 16 : (t + 1) * chunk, :] for t in range(8)], axis=0
    )
    rank = basis.shape[1]
    width = mine_ref.shape[1]
    r, place = iota((rank, rank), 0), iota((rank, rank), 1)
    for half in range(2):
        in_half = ((place >> 2) & 1) == half
        own = one_hot((r == rank_of(place, core)) & in_half)
        other = one_hot((r == rank_of(place, 1 - core)) & in_half)
        own_basis = jnp.dot(basis, own, preferred_element_type=F32).astype(BF16)
        other_basis = jnp.dot(basis, other, preferred_element_type=F32).astype(BF16)
        tile = 256
        for start in range(0, width, tile):
            out_ref[:, half * width + start : half * width + start + tile] = (
                jnp.dot(
                    own_basis, mine_ref[:, start : start + tile], preferred_element_type=F32
                )
                + jnp.dot(
                    other_basis, theirs_ref[:, start : start + tile], preferred_element_type=F32
                )
            ).astype(BF16)


def per_device(tokens, grad_gate, basis, first_moment, second_moment):
    rows, features = tokens.shape
    own, rank = basis.shape
    group_tokens, columns = grad_gate.shape
    half = columns // 2
    scale = 1.0 / math.sqrt(group_tokens * Z * Y_LO * CORE)
    shape = jax.ShapeDtypeStruct
    core = lax.axis_index("core").astype(jnp.int32)
    at = jnp.stack([core, lax.axis_index("x").astype(jnp.int32)])
    sibling_at = jnp.stack([1 - core, lax.axis_index("x").astype(jnp.int32)])
    swap = [(0, 1), (1, 0)]

    def exchange(array, axes):
        return lax.all_to_all(array, axes, 0, 0, tiled=True)

    copies = Z * Y_LO * Y_HI
    basis_copies = jnp.broadcast_to(basis[None], (copies, own, rank))
    class_basis = exchange(basis_copies, ("z", "y_lo", "y_hi")).reshape(copies * own, rank)
    side = shape((rows, features // CORE), BF16)
    blocks_sem = pltpu.SemaphoreType.DMA((Z * Y_LO,))
    for_sibling = call(take_sibling, side, 0, 2 * rows * features, "sh", [blocks_sem], MOST_VMEM)(at, tokens)
    sibling = lax.ppermute(for_sibling, "core", swap)
    block = shape((CORE * rows, features // CLASSES), BF16)
    blocks = call(
        split_features,
        (block,) * X,
        2 * rows * features * 512,
        0,
        "sh",
        [pltpu.VMEM(side.shape, BF16), blocks_sem],
        MOST_VMEM,
    )(at, tokens, sibling)
    held = [blocks[0]] + [
        lax.ppermute(blocks[step], "x", [(x, (x + step) % X) for x in range(X)])
        for step in range(1, X)
    ]
    parts = call(
        partial_coefficients,
        shape((CLASSES, rows, rank), F32),
        2 * rows * features * rank,
        2 * (rows * features + copies * own * rank),
        "svhhhh",
        [pltpu.VMEM((X,) + block.shape, BF16), pltpu.SemaphoreType.DMA((X,))],
        MOST_VMEM,
    )(at, class_basis, *held)
    parts = exchange(parts, ("core", "x"))
    takers = Y_HI * X
    chunk = rows + own
    gathered = exchange(
        call(
            sum_coefficients,
            shape((takers, chunk, rank), BF16),
            CLASSES * rows * rank,
            4 * takers * chunk * rank,
        )(parts, basis),
        ("y_hi", "x"),
    ).reshape(takers * chunk, rank)

    def projected(which, dtype):
        return call(
            functools.partial(project, scale),
            shape((rank, half), dtype),
            2 * rank * group_tokens * columns,
            2 * group_tokens * columns + 2 * rank * columns,
            "s",
        )(which, gathered, grad_gate)

    theirs = lax.ppermute(projected(sibling_at, BF16), "core", swap)
    mine = projected(at, F32)
    pair = call(add_halves, shape((rank, half), BF16), rank * half, 8 * rank * half)(mine, theirs)
    owned = exchange(pair, ("z", "y_lo"))
    first_out, second_out, direction = call(
        adam,
        (
            shape(first_moment.shape, F32),
            shape(second_moment.shape, F32),
            shape((rank, half), BF16),
        ),
        rank * half,
        4 * rank * half,
    )(owned, first_moment, second_moment)
    directions = exchange(direction, ("z", "y_lo"))
    others = lax.ppermute(directions, "core", swap)
    update = call(
        expand,
        shape((own * takers, columns), BF16),
        4 * own * takers * rank * columns,
        4 * rank * columns,
        "s",
    )(at, gathered, directions, others)
    return (update, first_out, second_out)


def solution(mesh):
    names = ("z", "y_lo", "core", "y_hi", "x")
    fine = Mesh(mesh.devices.reshape(Z, Y_LO, CORE, Y_HI, X), names)
    data, tensor = names[:3], names[3:]
    placed = (P(names, None), P(data, tensor), P(names, None), P(data, tensor), P(data, tensor))
    return jax.shard_map(
        per_device,
        mesh=fine,
        in_specs=placed,
        out_specs=(P(data, tensor), P(data, tensor), P(data, tensor)),
        check_vma=False,
    )
```

```python
import functools
import math

import jax
import jax.numpy as jnp
from jax import lax
from jax.experimental import pallas as pl
from jax.experimental.pallas import tpu as pltpu
from jax.sharding import Mesh
from jax.sharding import PartitionSpec as P

STEP = 10


BETA_ONE = 0.9
BETA_TWO = 0.95
EPS = 1e-08

Z, Y_LO, CORE, Y_HI, X = 8, 4, 2, 2, 4
OWNERS = Z * Y_LO
VMEM_LIMIT = 24 * 1024 * 1024
F32, BF16 = jnp.float32, jnp.bfloat16


def call(body, out_shape, flops, moved, placed=False):
    vmem = pl.BlockSpec(memory_space=pltpu.VMEM)
    smem = pl.BlockSpec(memory_space=pltpu.SMEM)

    def run(*operands):
        specs = [smem if placed and n == 0 else vmem for n in range(len(operands))]
        return pl.pallas_call(
            body,
            out_shape=out_shape,
            in_specs=specs,
            out_specs=jax.tree.map(lambda _: vmem, out_shape),
            compiler_params=pltpu.CompilerParams(vmem_limit_bytes=VMEM_LIMIT),
            cost_estimate=pl.CostEstimate(flops=flops, bytes_accessed=moved, transcendentals=0),
        )(*operands)

    return run


def iota(shape, axis):
    return lax.broadcasted_iota(jnp.int32, shape, axis)


def one_hot(condition):
    return jnp.where(condition, 1.0, 0.0).astype(BF16)


def split_features(at_ref, tokens_ref, *out_refs):
    here = at_ref[1]
    width = Y_LO * 128
    p, q = iota((width, width), 0), iota((width, width), 1)
    steps = (((p >> 4) & 3) - here) & 3
    move = one_hot(steps * 128 + (p >> 7) * 32 + ((p >> 6) & 1) * 16 + (p & 15) == q)
    for z in range(Z):
        for side in range(CORE):
            block = jnp.concatenate(
                [
                    tokens_ref[:, ((z * Y_LO + y) * CORE + side) * 128 :][:, :128]
                    for y in range(Y_LO)
                ],
                axis=1,
            )
            moved = jnp.dot(block, move, preferred_element_type=F32).astype(BF16)
            start = (side * Z + z) * 128
            for x in range(X):
                out_refs[x][:, start : start + 128] = moved[:, x * 128 : (x + 1) * 128]


def class_part(token_refs, basis_ref, side):
    width = basis_ref.shape[0]
    columns = pl.ds(pl.multiple_of(side * width, 128), width)
    tokens = jnp.concatenate([ref[:, columns] for ref in token_refs], axis=0)
    return jnp.dot(tokens, basis_ref[...], preferred_element_type=F32)


def partial_coefficients(at_ref, basis_ref, *refs):
    *token_refs, out_ref = refs
    here, rows = at_ref[1], out_ref.shape[1]
    parts = class_part(token_refs, basis_ref, at_ref[0])
    for step in range(X):
        out_ref[(here - step) & 3] = parts[step * rows : (step + 1) * rows, :]


def whole_coefficients(at_ref, basis_ref, part_ref, *refs):
    *token_refs, out_ref = refs
    here, rows = at_ref[1], out_ref.shape[1]
    parts = class_part(token_refs, basis_ref, 1 - at_ref[0])
    for step in range(X):
        place = (here - step) & 3
        out_ref[place] = part_ref[place] + parts[step * rows : (step + 1) * rows, :]


def sum_coefficients(parts_ref, basis_ref, out_ref):
    rows = parts_ref.shape[1]
    own = basis_ref.shape[0]
    total = (parts_ref[0] + parts_ref[1]) + (parts_ref[2] + parts_ref[3])
    total = total.astype(BF16)
    basis = basis_ref[...]
    for copy in range(out_ref.shape[0]):
        out_ref[copy, 0:rows, :] = total
        out_ref[copy, rows : rows + own, :] = basis


def rank_of(row, core):
    return (row >> 3) * 8 + core * 4 + (row & 3)


def project(scale, core_ref, gathered_ref, grad_ref, out_ref):
    core = core_ref[0]
    width = out_ref.shape[1]
    chunk = gathered_ref.shape[0] // 8
    tokens = chunk - 16
    coefficients = jnp.concatenate(
        [gathered_ref[t * chunk : t * chunk + tokens, :] for t in range(8)], axis=0
    )
    rank = coefficients.shape[1]
    rows = out_ref.shape[0]
    place = one_hot(rank_of(iota((rows, rank), 0), core) == iota((rows, rank), 1))
    arranged = lax.dot_general(
        place, coefficients, (((1,), (1,)), ((), ())), preferred_element_type=F32
    ).astype(BF16)
    tile = 256
    first_half = (iota((rows, tile), 0) & 4) == 0
    for start in range(0, width, tile):
        low = jnp.dot(
            arranged, grad_ref[:, start : start + tile], preferred_element_type=F32
        )
        high = jnp.dot(
            arranged,
            grad_ref[:, width + start : width + start + tile],
            preferred_element_type=F32,
        )
        out_ref[:, start : start + tile] = (
            jnp.where(first_half, low, high) * scale
        ).astype(out_ref.dtype)


def add_halves(mine_ref, theirs_ref, out_ref):
    out_ref[...] = (mine_ref[...] + theirs_ref[...].astype(F32)).astype(BF16)


def adam(parts_ref, first_ref, second_ref, first_out_ref, second_out_ref, out_ref):
    rows, width = 4, parts_ref.shape[1]
    total = parts_ref[0:16, :].astype(F32)
    for part in range(1, parts_ref.shape[0] // 16):
        total += parts_ref[part * 16 : (part + 1) * 16, :].astype(F32)
    total = total[0:8, :] + total[8:16, :]
    directions = []
    for half in range(2):
        grad = total[half * rows : (half + 1) * rows, :]
        columns = slice(half * width, (half + 1) * width)
        first_out = BETA_ONE * first_ref[:, columns] + (1.0 - BETA_ONE) * grad
        second_out = BETA_TWO * second_ref[:, columns] + (1.0 - BETA_TWO) * grad * grad
        first_out_ref[:, columns] = first_out
        second_out_ref[:, columns] = second_out
        corrected = first_out / (1.0 - BETA_ONE**STEP)
        scaled = jnp.sqrt(second_out / (1.0 - BETA_TWO**STEP)) + EPS
        directions.append(corrected / scaled)
    block = jnp.concatenate(directions + directions, axis=0).astype(BF16)
    for part in range(out_ref.shape[0] // 16):
        out_ref[part * 16 : (part + 1) * 16, :] = block


def expand(core_ref, gathered_ref, mine_ref, theirs_ref, out_ref):
    core = core_ref[0]
    chunk = gathered_ref.shape[0] // 8
    basis = jnp.concatenate(
        [gathered_ref[t * chunk + chunk - 16 : (t + 1) * chunk, :] for t in range(8)], axis=0
    )
    rank = basis.shape[1]
    width = mine_ref.shape[1]
    r, place = iota((rank, rank), 0), iota((rank, rank), 1)
    for half in range(2):
        in_half = ((place >> 2) & 1) == half
        own = one_hot((r == rank_of(place, core)) & in_half)
        other = one_hot((r == rank_of(place, 1 - core)) & in_half)
        own_basis = jnp.dot(basis, own, preferred_element_type=F32).astype(BF16)
        other_basis = jnp.dot(basis, other, preferred_element_type=F32).astype(BF16)
        tile = 256
        for start in range(0, width, tile):
            out_ref[:, half * width + start : half * width + start + tile] = (
                jnp.dot(
                    own_basis, mine_ref[:, start : start + tile], preferred_element_type=F32
                )
                + jnp.dot(
                    other_basis, theirs_ref[:, start : start + tile], preferred_element_type=F32
                )
            ).astype(BF16)


def per_device(tokens, grad_gate, basis, first_moment, second_moment):
    rows, features = tokens.shape
    own, rank = basis.shape
    group_tokens, columns = grad_gate.shape
    half = columns // 2
    scale = 1.0 / math.sqrt(group_tokens * Z * Y_LO * CORE)
    shape = jax.ShapeDtypeStruct
    core = lax.axis_index("core").astype(jnp.int32)
    at = jnp.stack([core, lax.axis_index("x").astype(jnp.int32)])
    sibling_at = jnp.stack([1 - core, lax.axis_index("x").astype(jnp.int32)])
    swap = [(0, 1), (1, 0)]

    def exchange(array, axes):
        return lax.all_to_all(array, axes, 0, 0, tiled=True)

    copies = Z * Y_LO * Y_HI
    basis_copies = jnp.broadcast_to(basis[None], (copies, own, rank))
    class_basis = exchange(basis_copies, ("z", "y_lo", "y_hi")).reshape(copies * own, rank)
    block = shape((rows, features // X), BF16)
    blocks = call(split_features, (block,) * X, 2 * rows * features * 512, 0, True)(at, tokens)
    held = [blocks[0]] + [
        lax.ppermute(blocks[step], "x", [(x, (x + step) % X) for x in range(X)])
        for step in range(1, X)
    ]
    class_basis, *held = lax.optimization_barrier((class_basis, *held))
    sibling_basis = lax.ppermute(class_basis, "core", swap)
    part_shape = shape((X, rows, rank), F32)
    part_cost = (rows * features * rank, rows * features + copies * own * rank)
    part = call(partial_coefficients, part_shape, *part_cost, True)(at, class_basis, *held)
    parts = call(whole_coefficients, part_shape, *part_cost, True)(
        at, sibling_basis, part, *held
    )
    parts = exchange(parts, "x")
    takers = Y_HI * X
    chunk = rows + own
    gathered = exchange(
        call(
            sum_coefficients,
            shape((takers, chunk, rank), BF16),
            X * rows * rank,
            4 * takers * chunk * rank,
        )(parts, basis),
        ("y_hi", "x"),
    ).reshape(takers * chunk, rank)

    def projected(which, dtype):
        return call(
            functools.partial(project, scale),
            shape((rank, half), dtype),
            2 * rank * group_tokens * columns,
            2 * group_tokens * columns + 2 * rank * columns,
            True,
        )(which, gathered, grad_gate)

    theirs = lax.ppermute(projected(sibling_at, BF16), "core", swap)
    mine = projected(at, F32)
    pair = call(add_halves, shape((rank, half), BF16), rank * half, 8 * rank * half)(mine, theirs)
    owned = exchange(pair, ("z", "y_lo"))
    first_out, second_out, direction = call(
        adam,
        (
            shape(first_moment.shape, F32),
            shape(second_moment.shape, F32),
            shape((rank, half), BF16),
        ),
        rank * half,
        4 * rank * half,
    )(owned, first_moment, second_moment)
    directions = exchange(direction, ("z", "y_lo"))
    others = lax.ppermute(directions, "core", swap)
    update = call(
        expand,
        shape((own * takers, columns), BF16),
        4 * own * takers * rank * columns,
        4 * rank * columns,
        True,
    )(at, gathered, directions, others)
    return (update, first_out, second_out)


def solution(mesh):
    names = ("z", "y_lo", "core", "y_hi", "x")
    fine = Mesh(mesh.devices.reshape(Z, Y_LO, CORE, Y_HI, X), names)
    data, tensor = names[:3], names[3:]
    placed = (P(names, None), P(data, tensor), P(names, None), P(data, tensor), P(data, tensor))
    return jax.shard_map(
        per_device,
        mesh=fine,
        in_specs=placed,
        out_specs=(P(data, tensor), P(data, tensor), P(data, tensor)),
        check_vma=False,
    )
```

```python
import functools
import math

import jax
import jax.numpy as jnp
from jax import lax
from jax.experimental import pallas as pl
from jax.experimental.pallas import tpu as pltpu
from jax.sharding import Mesh
from jax.sharding import PartitionSpec as P

STEP = 10


BETA_ONE = 0.9
BETA_TWO = 0.95
EPS = 1e-08

Z, Y_LO, CORE, Y_HI, X = 8, 4, 2, 2, 4
OWNERS = Z * Y_LO
VMEM_LIMIT = 24 * 1024 * 1024
F32, BF16 = jnp.float32, jnp.bfloat16


def call(body, out_shape, flops, moved):
    return pl.pallas_call(
        body,
        out_shape=out_shape,
        compiler_params=pltpu.CompilerParams(vmem_limit_bytes=VMEM_LIMIT),
        cost_estimate=pl.CostEstimate(flops=flops, bytes_accessed=moved, transcendentals=0),
    )


def iota(shape, axis):
    return lax.broadcasted_iota(jnp.int32, shape, axis)


def one_hot(condition):
    return jnp.where(condition, 1.0, 0.0).astype(BF16)


def split_features(tokens_ref, *out_refs):
    here = lax.axis_index("x")
    width = Y_LO * 128
    p, q = iota((width, width), 0), iota((width, width), 1)
    steps = (((p >> 4) & 3) - here) & 3
    move = one_hot(steps * 128 + (p >> 7) * 32 + ((p >> 6) & 1) * 16 + (p & 15) == q)
    for z in range(Z):
        for side in range(CORE):
            block = jnp.concatenate(
                [
                    tokens_ref[:, pl.ds(((z * Y_LO + y) * CORE + side) * 128, 128)]
                    for y in range(Y_LO)
                ],
                axis=1,
            )
            moved = jnp.dot(block, move, preferred_element_type=F32).astype(BF16)
            start = (side * Z + z) * 128
            for x in range(X):
                out_refs[x][:, start : start + 128] = moved[:, x * 128 : (x + 1) * 128]


def class_part(token_refs, basis_ref, side):
    width = basis_ref.shape[0]
    columns = pl.ds(pl.multiple_of(side * width, 128), width)
    tokens = jnp.concatenate([ref[:, columns] for ref in token_refs], axis=0)
    return jnp.dot(tokens, basis_ref[...], preferred_element_type=F32)


def partial_coefficients(basis_ref, *refs):
    *token_refs, out_ref = refs
    here, rows = lax.axis_index("x"), out_ref.shape[1]
    parts = class_part(token_refs, basis_ref, lax.axis_index("core"))
    for step in range(X):
        out_ref[(here - step) & 3] = parts[step * rows : (step + 1) * rows, :]


def whole_coefficients(basis_ref, part_ref, *refs):
    *token_refs, out_ref = refs
    here, rows = lax.axis_index("x"), out_ref.shape[1]
    parts = class_part(token_refs, basis_ref, 1 - lax.axis_index("core"))
    for step in range(X):
        place = (here - step) & 3
        out_ref[place] = part_ref[place] + parts[step * rows : (step + 1) * rows, :]


def sum_coefficients(parts_ref, basis_ref, out_ref):
    rows = parts_ref.shape[1]
    own = basis_ref.shape[0]
    total = (parts_ref[0] + parts_ref[1]) + (parts_ref[2] + parts_ref[3])
    total = total.astype(BF16)
    basis = basis_ref[...]
    for copy in range(out_ref.shape[0]):
        out_ref[copy, 0:rows, :] = total
        out_ref[copy, rows : rows + own, :] = basis


def rank_of(row, core):
    return (row >> 3) * 8 + core * 4 + (row & 3)


def project(scale, own, gathered_ref, grad_ref, out_ref):
    core = lax.axis_index("core")
    core = core if own else 1 - core
    width = out_ref.shape[1]
    chunk = gathered_ref.shape[0] // 8
    tokens = chunk - 16
    coefficients = jnp.concatenate(
        [gathered_ref[t * chunk : t * chunk + tokens, :] for t in range(8)], axis=0
    )
    rank = coefficients.shape[1]
    rows = out_ref.shape[0]
    place = one_hot(rank_of(iota((rows, rank), 0), core) == iota((rows, rank), 1))
    arranged = lax.dot_general(
        place, coefficients, (((1,), (1,)), ((), ())), preferred_element_type=F32
    ).astype(BF16)
    tile = 256
    first_half = (iota((rows, tile), 0) & 4) == 0
    for start in range(0, width, tile):
        low = jnp.dot(
            arranged, grad_ref[:, start : start + tile], preferred_element_type=F32
        )
        high = jnp.dot(
            arranged,
            grad_ref[:, width + start : width + start + tile],
            preferred_element_type=F32,
        )
        out_ref[:, start : start + tile] = (
            jnp.where(first_half, low, high) * scale
        ).astype(out_ref.dtype)


def add_halves(mine_ref, theirs_ref, out_ref):
    out_ref[...] = (mine_ref[...] + theirs_ref[...].astype(F32)).astype(BF16)


def adam(parts_ref, first_ref, second_ref, first_out_ref, second_out_ref, out_ref):
    rows, width = 4, parts_ref.shape[1]
    total = parts_ref[0:16, :].astype(F32)
    for part in range(1, parts_ref.shape[0] // 16):
        total += parts_ref[part * 16 : (part + 1) * 16, :].astype(F32)
    total = total[0:8, :] + total[8:16, :]
    directions = []
    for half in range(2):
        grad = total[half * rows : (half + 1) * rows, :]
        columns = slice(half * width, (half + 1) * width)
        first_out = BETA_ONE * first_ref[:, columns] + (1.0 - BETA_ONE) * grad
        second_out = BETA_TWO * second_ref[:, columns] + (1.0 - BETA_TWO) * grad * grad
        first_out_ref[:, columns] = first_out
        second_out_ref[:, columns] = second_out
        corrected = first_out / (1.0 - BETA_ONE**STEP)
        scaled = jnp.sqrt(second_out / (1.0 - BETA_TWO**STEP)) + EPS
        directions.append(corrected / scaled)
    block = jnp.concatenate(directions + directions, axis=0).astype(BF16)
    for part in range(out_ref.shape[0] // 16):
        out_ref[part * 16 : (part + 1) * 16, :] = block


def expand(gathered_ref, mine_ref, theirs_ref, out_ref):
    core = lax.axis_index("core")
    chunk = gathered_ref.shape[0] // 8
    basis = jnp.concatenate(
        [gathered_ref[t * chunk + chunk - 16 : (t + 1) * chunk, :] for t in range(8)], axis=0
    )
    rank = basis.shape[1]
    width = mine_ref.shape[1]
    r, place = iota((rank, rank), 0), iota((rank, rank), 1)
    for half in range(2):
        in_half = ((place >> 2) & 1) == half
        own = one_hot((r == rank_of(place, core)) & in_half)
        other = one_hot((r == rank_of(place, 1 - core)) & in_half)
        own_basis = jnp.dot(basis, own, preferred_element_type=F32).astype(BF16)
        other_basis = jnp.dot(basis, other, preferred_element_type=F32).astype(BF16)
        tile = 256
        for start in range(0, width, tile):
            out_ref[:, half * width + start : half * width + start + tile] = (
                jnp.dot(
                    own_basis, mine_ref[:, start : start + tile], preferred_element_type=F32
                )
                + jnp.dot(
                    other_basis, theirs_ref[:, start : start + tile], preferred_element_type=F32
                )
            ).astype(BF16)


def per_device(tokens, grad_gate, basis, first_moment, second_moment):
    rows, features = tokens.shape
    own, rank = basis.shape
    group_tokens, columns = grad_gate.shape
    half = columns // 2
    scale = 1.0 / math.sqrt(group_tokens * Z * Y_LO * CORE)
    shape = jax.ShapeDtypeStruct
    swap = [(0, 1), (1, 0)]

    def exchange(array, axes):
        return lax.all_to_all(array, axes, 0, 0, tiled=True)

    copies = Z * Y_LO * Y_HI
    basis_copies = jnp.broadcast_to(basis[None], (copies, own, rank))
    class_basis = exchange(basis_copies, ("z", "y_lo", "y_hi")).reshape(copies * own, rank)
    block = shape((rows, features // X), BF16)
    blocks = call(split_features, (block,) * X, 2 * rows * features * 512, 0)(tokens)
    held = [blocks[0]] + [
        lax.ppermute(blocks[step], "x", [(x, (x + step) % X) for x in range(X)])
        for step in range(1, X)
    ]
    class_basis, *held = lax.optimization_barrier((class_basis, *held))
    sibling_basis = lax.ppermute(class_basis, "core", swap)
    part_shape = shape((X, rows, rank), F32)
    part_cost = (rows * features * rank, rows * features + copies * own * rank)
    part = call(partial_coefficients, part_shape, *part_cost)(class_basis, *held)
    parts = call(whole_coefficients, part_shape, *part_cost)(
        sibling_basis, part, *held
    )
    parts = exchange(parts, "x")
    takers = Y_HI * X
    chunk = rows + own
    gathered = exchange(
        call(
            sum_coefficients,
            shape((takers, chunk, rank), BF16),
            X * rows * rank,
            4 * takers * chunk * rank,
        )(parts, basis),
        ("y_hi", "x"),
    ).reshape(takers * chunk, rank)

    def projected(own_half, dtype):
        return call(
            functools.partial(project, scale, own_half),
            shape((rank, half), dtype),
            2 * rank * group_tokens * columns,
            2 * group_tokens * columns + 2 * rank * columns,
            )(gathered, grad_gate)

    theirs = lax.ppermute(projected(False, BF16), "core", swap)
    mine = projected(True, F32)
    pair = call(add_halves, shape((rank, half), BF16), rank * half, 8 * rank * half)(mine, theirs)
    owned = exchange(pair, ("z", "y_lo"))
    first_out, second_out, direction = call(
        adam,
        (
            shape(first_moment.shape, F32),
            shape(second_moment.shape, F32),
            shape((rank, half), BF16),
        ),
        rank * half,
        4 * rank * half,
    )(owned, first_moment, second_moment)
    directions = exchange(direction, ("z", "y_lo"))
    others = lax.ppermute(directions, "core", swap)
    update = call(
        expand,
        shape((own * takers, columns), BF16),
        4 * own * takers * rank * columns,
        4 * rank * columns,
    )(gathered, directions, others)
    return (update, first_out, second_out)


def solution(mesh):
    names = ("z", "y_lo", "core", "y_hi", "x")
    fine = Mesh(mesh.devices.reshape(Z, Y_LO, CORE, Y_HI, X), names)
    data, tensor = names[:3], names[3:]
    placed = (P(names, None), P(data, tensor), P(names, None), P(data, tensor), P(data, tensor))
    return jax.shard_map(
        per_device,
        mesh=fine,
        in_specs=placed,
        out_specs=(P(data, tensor), P(data, tensor), P(data, tensor)),
        check_vma=False,
    )
```

```python
import functools
import math

import jax
import jax.numpy as jnp
from jax import lax
from jax.experimental import pallas as pl
from jax.experimental.pallas import tpu as pltpu
from jax.sharding import Mesh
from jax.sharding import PartitionSpec as P

STEP = 10


BETA_ONE = 0.9
BETA_TWO = 0.95
EPS = 1e-08

Z, Y_LO, CORE, Y_HI, X = 8, 4, 2, 2, 4
OWNERS = Z * Y_LO
VMEM_LIMIT = 24 * 1024 * 1024
F32, BF16 = jnp.float32, jnp.bfloat16


def call(body, out_shape, flops, moved):
    return pl.pallas_call(
        body,
        out_shape=out_shape,
        compiler_params=pltpu.CompilerParams(vmem_limit_bytes=VMEM_LIMIT),
        cost_estimate=pl.CostEstimate(flops=flops, bytes_accessed=moved, transcendentals=0),
    )


def iota(shape, axis):
    return lax.broadcasted_iota(jnp.int32, shape, axis)


def one_hot(condition):
    return jnp.where(condition, 1.0, 0.0).astype(BF16)


def split_features(tokens_ref, *out_refs):
    here = lax.axis_index("x")
    width = Y_LO * 128
    p, q = iota((width, width), 0), iota((width, width), 1)
    steps = (((p >> 4) & 3) - here) & 3
    move = one_hot(steps * 128 + (p >> 7) * 32 + ((p >> 6) & 1) * 16 + (p & 15) == q)
    for z in range(Z):
        for side in range(CORE):
            block = jnp.concatenate(
                [
                    tokens_ref[:, pl.ds(((z * Y_LO + y) * CORE + side) * 128, 128)]
                    for y in range(Y_LO)
                ],
                axis=1,
            )
            moved = jnp.dot(block, move, preferred_element_type=F32).astype(BF16)
            start = (side * Z + z) * 128
            for x in range(X):
                out_refs[x][:, start : start + 128] = moved[:, x * 128 : (x + 1) * 128]


def stack(*refs):
    *block_refs, out_ref = refs
    rows = block_refs[0].shape[0]
    for step, ref in enumerate(block_refs):
        out_ref[step * rows : (step + 1) * rows, :] = ref[...]


def class_part(tokens_ref, basis_ref, side):
    width = basis_ref.shape[0]
    columns = pl.ds(pl.multiple_of(side * width, 128), width)
    return jnp.dot(tokens_ref[:, columns], basis_ref[...], preferred_element_type=F32)


def partial_coefficients(basis_ref, tokens_ref, out_ref):
    here, rows = lax.axis_index("x"), out_ref.shape[1]
    parts = class_part(tokens_ref, basis_ref, lax.axis_index("core"))
    for step in range(X):
        out_ref[(here - step) & 3] = parts[step * rows : (step + 1) * rows, :]


def whole_coefficients(basis_ref, part_ref, tokens_ref, out_ref):
    here, rows = lax.axis_index("x"), out_ref.shape[1]
    parts = class_part(tokens_ref, basis_ref, 1 - lax.axis_index("core"))
    for step in range(X):
        place = (here - step) & 3
        out_ref[place] = part_ref[place] + parts[step * rows : (step + 1) * rows, :]


def sum_coefficients(parts_ref, basis_ref, out_ref):
    rows = parts_ref.shape[1]
    own = basis_ref.shape[0]
    total = (parts_ref[0] + parts_ref[1]) + (parts_ref[2] + parts_ref[3])
    total = total.astype(BF16)
    basis = basis_ref[...]
    for copy in range(out_ref.shape[0]):
        out_ref[copy, 0:rows, :] = total
        out_ref[copy, rows : rows + own, :] = basis


def rank_of(row, core):
    return (row >> 3) * 8 + core * 4 + (row & 3)


def project(scale, own, gathered_ref, grad_ref, out_ref):
    core = lax.axis_index("core")
    core = core if own else 1 - core
    width = out_ref.shape[1]
    chunk = gathered_ref.shape[0] // 8
    tokens = chunk - 16
    coefficients = jnp.concatenate(
        [gathered_ref[t * chunk : t * chunk + tokens, :] for t in range(8)], axis=0
    )
    rank = coefficients.shape[1]
    rows = out_ref.shape[0]
    place = one_hot(rank_of(iota((rows, rank), 0), core) == iota((rows, rank), 1))
    arranged = lax.dot_general(
        place, coefficients, (((1,), (1,)), ((), ())), preferred_element_type=F32
    ).astype(BF16)
    tile = 256
    first_half = (iota((rows, tile), 0) & 4) == 0
    for start in range(0, width, tile):
        low = jnp.dot(
            arranged, grad_ref[:, start : start + tile], preferred_element_type=F32
        )
        high = jnp.dot(
            arranged,
            grad_ref[:, width + start : width + start + tile],
            preferred_element_type=F32,
        )
        out_ref[:, start : start + tile] = (
            jnp.where(first_half, low, high) * scale
        ).astype(out_ref.dtype)


def add_halves(mine_ref, theirs_ref, out_ref):
    out_ref[...] = (mine_ref[...] + theirs_ref[...].astype(F32)).astype(BF16)


def adam(parts_ref, first_ref, second_ref, first_out_ref, second_out_ref, out_ref):
    rows, width = 4, parts_ref.shape[1]
    total = parts_ref[0:16, :].astype(F32)
    for part in range(1, parts_ref.shape[0] // 16):
        total += parts_ref[part * 16 : (part + 1) * 16, :].astype(F32)
    total = total[0:8, :] + total[8:16, :]
    directions = []
    for half in range(2):
        grad = total[half * rows : (half + 1) * rows, :]
        columns = slice(half * width, (half + 1) * width)
        first_out = BETA_ONE * first_ref[:, columns] + (1.0 - BETA_ONE) * grad
        second_out = BETA_TWO * second_ref[:, columns] + (1.0 - BETA_TWO) * grad * grad
        first_out_ref[:, columns] = first_out
        second_out_ref[:, columns] = second_out
        corrected = first_out / (1.0 - BETA_ONE**STEP)
        scaled = jnp.sqrt(second_out / (1.0 - BETA_TWO**STEP)) + EPS
        directions.append(corrected / scaled)
    block = jnp.concatenate(directions + directions, axis=0).astype(BF16)
    for part in range(out_ref.shape[0] // 16):
        out_ref[part * 16 : (part + 1) * 16, :] = block


def arrange_basis(gathered_ref, out_ref):
    core = lax.axis_index("core")
    chunk = gathered_ref.shape[0] // 8
    basis = jnp.concatenate(
        [gathered_ref[t * chunk + chunk - 16 : (t + 1) * chunk, :] for t in range(8)], axis=0
    )
    rank = basis.shape[1]
    r, place = iota((rank, rank), 0), iota((rank, rank), 1)
    for which in range(CORE):
        side = core if which == 0 else 1 - core
        for half in range(2):
            move = one_hot((r == rank_of(place, side)) & (((place >> 2) & 1) == half))
            out_ref[2 * which + half] = jnp.dot(
                basis, move, preferred_element_type=F32
            ).astype(BF16)


def expand_own(basis_ref, directions_ref, out_ref):
    width = directions_ref.shape[1]
    tile = 256
    for half in range(2):
        basis = basis_ref[half]
        for start in range(0, width, tile):
            out_ref[:, half * width + start : half * width + start + tile] = jnp.dot(
                basis, directions_ref[:, start : start + tile], preferred_element_type=F32
            )


def expand(basis_ref, part_ref, directions_ref, out_ref):
    width = directions_ref.shape[1]
    tile = 256
    for half in range(2):
        basis = basis_ref[2 + half]
        for start in range(0, width, tile):
            columns = slice(half * width + start, half * width + start + tile)
            out_ref[:, columns] = (
                part_ref[:, columns]
                + jnp.dot(
                    basis, directions_ref[:, start : start + tile], preferred_element_type=F32
                )
            ).astype(BF16)


def per_device(tokens, grad_gate, basis, first_moment, second_moment):
    rows, features = tokens.shape
    own, rank = basis.shape
    group_tokens, columns = grad_gate.shape
    half = columns // 2
    scale = 1.0 / math.sqrt(group_tokens * Z * Y_LO * CORE)
    shape = jax.ShapeDtypeStruct
    swap = [(0, 1), (1, 0)]

    def exchange(array, axes):
        return lax.all_to_all(array, axes, 0, 0, tiled=True)

    copies = Z * Y_LO * Y_HI
    basis_copies = jnp.broadcast_to(basis[None], (copies, own, rank))
    class_basis = exchange(basis_copies, ("z", "y_lo", "y_hi")).reshape(copies * own, rank)
    block = shape((rows, features // X), BF16)
    blocks = call(split_features, (block,) * X, 2 * rows * features * 512, 0)(tokens)
    held = [blocks[0]] + [
        lax.ppermute(blocks[step], "x", [(x, (x + step) % X) for x in range(X)])
        for step in range(1, X)
    ]
    stacked = call(
        stack, shape((X * rows, features // X), BF16), rows * features, 4 * rows * features
    )(*held)
    class_basis, stacked = lax.optimization_barrier((class_basis, stacked))
    sibling_basis = lax.ppermute(class_basis, "core", swap)
    part_shape = shape((X, rows, rank), F32)
    part_cost = (rows * features * rank, rows * features + copies * own * rank)
    part = call(partial_coefficients, part_shape, *part_cost)(class_basis, stacked)
    parts = call(whole_coefficients, part_shape, *part_cost)(
        sibling_basis, part, stacked
    )
    parts = exchange(parts, "x")
    takers = Y_HI * X
    chunk = rows + own
    gathered = exchange(
        call(
            sum_coefficients,
            shape((takers, chunk, rank), BF16),
            X * rows * rank,
            4 * takers * chunk * rank,
        )(parts, basis),
        ("y_hi", "x"),
    ).reshape(takers * chunk, rank)

    def projected(own_half, dtype):
        return call(
            functools.partial(project, scale, own_half),
            shape((rank, half), dtype),
            2 * rank * group_tokens * columns,
            2 * group_tokens * columns + 2 * rank * columns,
            )(gathered, grad_gate)

    theirs = lax.ppermute(projected(False, BF16), "core", swap)
    mine = projected(True, F32)
    pair = call(add_halves, shape((rank, half), BF16), rank * half, 8 * rank * half)(mine, theirs)
    owned = exchange(pair, ("z", "y_lo"))
    first_out, second_out, direction = call(
        adam,
        (
            shape(first_moment.shape, F32),
            shape(second_moment.shape, F32),
            shape((rank, half), BF16),
        ),
        rank * half,
        4 * rank * half,
    )(owned, first_moment, second_moment)
    directions = exchange(direction, ("z", "y_lo"))
    others = lax.ppermute(directions, "core", swap)
    update_rows = own * takers
    bases = call(
        arrange_basis, shape((4, update_rows, rank), BF16), 8 * update_rows * rank * rank, 0
    )(gathered)
    cost = (4 * update_rows * rank * half, 4 * update_rows * columns)
    part = call(expand_own, shape((update_rows, columns), F32), *cost)(bases, directions)
    update = call(expand, shape((update_rows, columns), BF16), *cost)(bases, part, others)
    return (update, first_out, second_out)


def solution(mesh):
    names = ("z", "y_lo", "core", "y_hi", "x")
    fine = Mesh(mesh.devices.reshape(Z, Y_LO, CORE, Y_HI, X), names)
    data, tensor = names[:3], names[3:]
    placed = (P(names, None), P(data, tensor), P(names, None), P(data, tensor), P(data, tensor))
    return jax.shard_map(
        per_device,
        mesh=fine,
        in_specs=placed,
        out_specs=(P(data, tensor), P(data, tensor), P(data, tensor)),
        check_vma=False,
    )
```

```python
import functools
import math

import jax
import jax.numpy as jnp
from jax import lax
from jax.experimental import pallas as pl
from jax.experimental.pallas import tpu as pltpu
from jax.sharding import Mesh
from jax.sharding import PartitionSpec as P

STEP = 10


BETA_ONE = 0.9
BETA_TWO = 0.95
EPS = 1e-08

Z, Y_LO, CORE, Y_HI, X = 8, 4, 2, 2, 4
OWNERS = Z * Y_LO
VMEM_LIMIT = 24 * 1024 * 1024
F32, BF16 = jnp.float32, jnp.bfloat16


def call(body, out_shape, flops, moved):
    return pl.pallas_call(
        body,
        out_shape=out_shape,
        compiler_params=pltpu.CompilerParams(vmem_limit_bytes=VMEM_LIMIT),
        cost_estimate=pl.CostEstimate(flops=flops, bytes_accessed=moved, transcendentals=0),
    )


def iota(shape, axis):
    return lax.broadcasted_iota(jnp.int32, shape, axis)


def one_hot(condition):
    return jnp.where(condition, 1.0, 0.0).astype(BF16)


def split_features(tokens_ref, *out_refs):
    here = lax.axis_index("x")
    width = Y_LO * 128
    p, q = iota((width, width), 0), iota((width, width), 1)
    steps = (((p >> 4) & 3) - here) & 3
    move = one_hot(steps * 128 + (p >> 7) * 32 + ((p >> 6) & 1) * 16 + (p & 15) == q)
    for z in range(Z):
        for side in range(CORE):
            block = jnp.concatenate(
                [
                    tokens_ref[:, pl.ds(((z * Y_LO + y) * CORE + side) * 128, 128)]
                    for y in range(Y_LO)
                ],
                axis=1,
            )
            moved = jnp.dot(block, move, preferred_element_type=F32).astype(BF16)
            start = (side * Z + z) * 128
            for x in range(X):
                out_refs[x][:, start : start + 128] = moved[:, x * 128 : (x + 1) * 128]


def stack(*refs):
    *block_refs, out_ref = refs
    rows = block_refs[0].shape[0]
    for step, ref in enumerate(block_refs):
        out_ref[step * rows : (step + 1) * rows, :] = ref[...]


def class_part(tokens_ref, basis_ref, side):
    width = basis_ref.shape[0]
    columns = pl.ds(pl.multiple_of(side * width, 128), width)
    return jnp.dot(tokens_ref[:, columns], basis_ref[...], preferred_element_type=F32)


def partial_coefficients(basis_ref, tokens_ref, out_ref):
    here, rows = lax.axis_index("x"), out_ref.shape[1]
    parts = class_part(tokens_ref, basis_ref, lax.axis_index("core"))
    for step in range(X):
        out_ref[(here - step) & 3] = parts[step * rows : (step + 1) * rows, :]


def whole_coefficients(basis_ref, part_ref, tokens_ref, out_ref):
    here, rows = lax.axis_index("x"), out_ref.shape[1]
    parts = class_part(tokens_ref, basis_ref, 1 - lax.axis_index("core"))
    for step in range(X):
        place = (here - step) & 3
        out_ref[place] = part_ref[place] + parts[step * rows : (step + 1) * rows, :]


def sum_coefficients(parts_ref, basis_ref, out_ref):
    rows = parts_ref.shape[1]
    own = basis_ref.shape[0]
    total = (parts_ref[0] + parts_ref[1]) + (parts_ref[2] + parts_ref[3])
    total = total.astype(BF16)
    basis = basis_ref[...]
    for copy in range(out_ref.shape[0]):
        out_ref[copy, 0:rows, :] = total
        out_ref[copy, rows : rows + own, :] = basis


def rank_of(row, core):
    return (row >> 3) * 8 + core * 4 + (row & 3)


def project(scale, own, gathered_ref, grad_ref, out_ref):
    core = lax.axis_index("core")
    core = core if own else 1 - core
    width = out_ref.shape[1]
    chunk = gathered_ref.shape[0] // 8
    tokens = chunk - 16
    coefficients = jnp.concatenate(
        [gathered_ref[t * chunk : t * chunk + tokens, :] for t in range(8)], axis=0
    )
    rank = coefficients.shape[1]
    rows = out_ref.shape[0]
    place = one_hot(rank_of(iota((rows, rank), 0), core) == iota((rows, rank), 1))
    arranged = lax.dot_general(
        place, coefficients, (((1,), (1,)), ((), ())), preferred_element_type=F32
    ).astype(BF16)
    tile = 256
    first_half = (iota((rows, tile), 0) & 4) == 0
    for start in range(0, width, tile):
        low = jnp.dot(
            arranged, grad_ref[:, start : start + tile], preferred_element_type=F32
        )
        high = jnp.dot(
            arranged,
            grad_ref[:, width + start : width + start + tile],
            preferred_element_type=F32,
        )
        out_ref[:, start : start + tile] = (
            jnp.where(first_half, low, high) * scale
        ).astype(out_ref.dtype)


def add_halves(mine_ref, theirs_ref, out_ref):
    out_ref[...] = (mine_ref[...] + theirs_ref[...].astype(F32)).astype(BF16)


def sum_planes(parts_ref, out_ref):
    total = parts_ref[0].astype(F32)
    for part in range(1, parts_ref.shape[0]):
        total += parts_ref[part].astype(F32)
    out_ref[...] = total.astype(BF16)


def repeat(block_ref, out_ref):
    block = block_ref[...]
    for copy in range(out_ref.shape[0]):
        out_ref[copy] = block


def adam(parts_ref, first_ref, second_ref, first_out_ref, second_out_ref, out_ref):
    rows, width = 4, parts_ref.shape[1]
    total = parts_ref[0:16, :].astype(F32)
    for part in range(1, parts_ref.shape[0] // 16):
        total += parts_ref[part * 16 : (part + 1) * 16, :].astype(F32)
    total = total[0:8, :] + total[8:16, :]
    directions = []
    for half in range(2):
        grad = total[half * rows : (half + 1) * rows, :]
        columns = slice(half * width, (half + 1) * width)
        first_out = BETA_ONE * first_ref[:, columns] + (1.0 - BETA_ONE) * grad
        second_out = BETA_TWO * second_ref[:, columns] + (1.0 - BETA_TWO) * grad * grad
        first_out_ref[:, columns] = first_out
        second_out_ref[:, columns] = second_out
        corrected = first_out / (1.0 - BETA_ONE**STEP)
        scaled = jnp.sqrt(second_out / (1.0 - BETA_TWO**STEP)) + EPS
        directions.append(corrected / scaled)
    block = jnp.concatenate(directions + directions, axis=0).astype(BF16)
    for part in range(out_ref.shape[0] // 16):
        out_ref[part * 16 : (part + 1) * 16, :] = block


def arrange_basis(gathered_ref, out_ref):
    core = lax.axis_index("core")
    chunk = gathered_ref.shape[0] // 8
    basis = jnp.concatenate(
        [gathered_ref[t * chunk + chunk - 16 : (t + 1) * chunk, :] for t in range(8)], axis=0
    )
    rank = basis.shape[1]
    r, place = iota((rank, rank), 0), iota((rank, rank), 1)
    for which in range(CORE):
        side = core if which == 0 else 1 - core
        for half in range(2):
            move = one_hot((r == rank_of(place, side)) & (((place >> 2) & 1) == half))
            out_ref[2 * which + half] = jnp.dot(
                basis, move, preferred_element_type=F32
            ).astype(BF16)


def expand_own(basis_ref, directions_ref, out_ref):
    width = directions_ref.shape[1]
    tile = 256
    for half in range(2):
        basis = basis_ref[half]
        for start in range(0, width, tile):
            out_ref[:, half * width + start : half * width + start + tile] = jnp.dot(
                basis, directions_ref[:, start : start + tile], preferred_element_type=F32
            )


def expand(basis_ref, part_ref, directions_ref, out_ref):
    width = directions_ref.shape[1]
    tile = 256
    for half in range(2):
        basis = basis_ref[2 + half]
        for start in range(0, width, tile):
            columns = slice(half * width + start, half * width + start + tile)
            out_ref[:, columns] = (
                part_ref[:, columns]
                + jnp.dot(
                    basis, directions_ref[:, start : start + tile], preferred_element_type=F32
                )
            ).astype(BF16)


def per_device(tokens, grad_gate, basis, first_moment, second_moment):
    rows, features = tokens.shape
    own, rank = basis.shape
    group_tokens, columns = grad_gate.shape
    half = columns // 2
    scale = 1.0 / math.sqrt(group_tokens * Z * Y_LO * CORE)
    shape = jax.ShapeDtypeStruct
    swap = [(0, 1), (1, 0)]

    def exchange(array, axes):
        return lax.all_to_all(array, axes, 0, 0, tiled=True)

    copies = Z * Y_LO * Y_HI
    basis_copies = jnp.broadcast_to(basis[None], (copies, own, rank))
    class_basis = exchange(basis_copies, ("z", "y_lo", "y_hi")).reshape(copies * own, rank)
    block = shape((rows, features // X), BF16)
    blocks = call(split_features, (block,) * X, 2 * rows * features * 512, 0)(tokens)
    held = [blocks[0]] + [
        lax.ppermute(blocks[step], "x", [(x, (x + step) % X) for x in range(X)])
        for step in range(1, X)
    ]
    stacked = call(
        stack, shape((X * rows, features // X), BF16), rows * features, 4 * rows * features
    )(*held)
    class_basis, stacked = lax.optimization_barrier((class_basis, stacked))
    sibling_basis = lax.ppermute(class_basis, "core", swap)
    part_shape = shape((X, rows, rank), F32)
    part_cost = (rows * features * rank, rows * features + copies * own * rank)
    part = call(partial_coefficients, part_shape, *part_cost)(class_basis, stacked)
    parts = call(whole_coefficients, part_shape, *part_cost)(
        sibling_basis, part, stacked
    )
    parts = exchange(parts, "x")
    takers = Y_HI * X
    chunk = rows + own
    gathered = exchange(
        call(
            sum_coefficients,
            shape((takers, chunk, rank), BF16),
            X * rows * rank,
            4 * takers * chunk * rank,
        )(parts, basis),
        ("y_hi", "x"),
    ).reshape(takers * chunk, rank)

    def projected(own_half, dtype):
        return call(
            functools.partial(project, scale, own_half),
            shape((rank, half), dtype),
            2 * rank * group_tokens * columns,
            2 * group_tokens * columns + 2 * rank * columns,
            )(gathered, grad_gate)

    theirs = lax.ppermute(projected(False, BF16), "core", swap)
    mine = projected(True, F32)
    pair = call(add_halves, shape((rank, half), BF16), rank * half, 8 * rank * half)(mine, theirs)
    plane = rank // Z
    planes = exchange(pair.reshape(Z, plane, half), "z")
    summed = call(sum_planes, shape((plane, half), BF16), rank * half, 2 * rank * half)(planes)
    owned = exchange(summed, "y_lo")
    first_out, second_out, direction = call(
        adam,
        (
            shape(first_moment.shape, F32),
            shape(second_moment.shape, F32),
            shape((plane, half), BF16),
        ),
        rank * half,
        4 * rank * half,
    )(owned, first_moment, second_moment)
    line = exchange(direction, "y_lo")
    planes = call(repeat, shape((Z, plane, half), BF16), 0, 2 * rank * half)(line)
    directions = exchange(planes, "z").reshape(rank, half)
    others = lax.ppermute(directions, "core", swap)
    update_rows = own * takers
    bases = call(
        arrange_basis, shape((4, update_rows, rank), BF16), 8 * update_rows * rank * rank, 0
    )(gathered)
    cost = (4 * update_rows * rank * half, 4 * update_rows * columns)
    part = call(expand_own, shape((update_rows, columns), F32), *cost)(bases, directions)
    update = call(expand, shape((update_rows, columns), BF16), *cost)(bases, part, others)
    return (update, first_out, second_out)


def solution(mesh):
    names = ("z", "y_lo", "core", "y_hi", "x")
    fine = Mesh(mesh.devices.reshape(Z, Y_LO, CORE, Y_HI, X), names)
    data, tensor = names[:3], names[3:]
    placed = (P(names, None), P(data, tensor), P(names, None), P(data, tensor), P(data, tensor))
    return jax.shard_map(
        per_device,
        mesh=fine,
        in_specs=placed,
        out_specs=(P(data, tensor), P(data, tensor), P(data, tensor)),
        check_vma=False,
    )
```

```python
import functools
import math

import jax
import jax.numpy as jnp
from jax import lax
from jax.experimental import pallas as pl
from jax.experimental.pallas import tpu as pltpu
from jax.sharding import Mesh
from jax.sharding import PartitionSpec as P

STEP = 10


BETA_ONE = 0.9
BETA_TWO = 0.95
EPS = 1e-08

Z, Y_LO, CORE, Y_HI, X = 8, 4, 2, 2, 4
OWNERS = Z * Y_LO
VMEM_LIMIT = 24 * 1024 * 1024
F32, BF16 = jnp.float32, jnp.bfloat16


def call(body, out_shape, flops, moved):
    return pl.pallas_call(
        body,
        out_shape=out_shape,
        compiler_params=pltpu.CompilerParams(vmem_limit_bytes=VMEM_LIMIT),
        cost_estimate=pl.CostEstimate(flops=flops, bytes_accessed=moved, transcendentals=0),
    )


def iota(shape, axis):
    return lax.broadcasted_iota(jnp.int32, shape, axis)


def one_hot(condition):
    return jnp.where(condition, 1.0, 0.0).astype(BF16)


def split_features(tokens_ref, *out_refs):
    here = lax.axis_index("x")
    width = Y_LO * 128
    p, q = iota((width, width), 0), iota((width, width), 1)
    steps = (((p >> 4) & 3) - here) & 3
    move = one_hot(steps * 128 + (p >> 7) * 32 + ((p >> 6) & 1) * 16 + (p & 15) == q)
    for z in range(Z):
        for side in range(CORE):
            block = jnp.concatenate(
                [
                    tokens_ref[:, pl.ds(((z * Y_LO + y) * CORE + side) * 128, 128)]
                    for y in range(Y_LO)
                ],
                axis=1,
            )
            moved = jnp.dot(block, move, preferred_element_type=F32).astype(BF16)
            start = (side * Z + z) * 128
            for x in range(X):
                out_refs[x][:, start : start + 128] = moved[:, x * 128 : (x + 1) * 128]


def stack(*refs):
    *block_refs, out_ref = refs
    rows = block_refs[0].shape[0]
    for step, ref in enumerate(block_refs):
        out_ref[step * rows : (step + 1) * rows, :] = ref[...]


def class_part(tokens_ref, basis_ref, side):
    width = basis_ref.shape[0]
    columns = pl.ds(pl.multiple_of(side * width, 128), width)
    return jnp.dot(tokens_ref[:, columns], basis_ref[...], preferred_element_type=F32)


def partial_coefficients(basis_ref, tokens_ref, out_ref):
    here, rows = lax.axis_index("x"), out_ref.shape[1]
    parts = class_part(tokens_ref, basis_ref, lax.axis_index("core"))
    for step in range(X):
        out_ref[(here - step) & 3] = parts[step * rows : (step + 1) * rows, :]


def whole_coefficients(basis_ref, part_ref, tokens_ref, out_ref):
    here, rows = lax.axis_index("x"), out_ref.shape[1]
    parts = class_part(tokens_ref, basis_ref, 1 - lax.axis_index("core"))
    for step in range(X):
        place = (here - step) & 3
        out_ref[place] = part_ref[place] + parts[step * rows : (step + 1) * rows, :]


def sum_coefficients(parts_ref, basis_ref, out_ref):
    rows = parts_ref.shape[1]
    own = basis_ref.shape[0]
    total = (parts_ref[0] + parts_ref[1]) + (parts_ref[2] + parts_ref[3])
    total = total.astype(BF16)
    basis = basis_ref[...]
    for copy in range(out_ref.shape[0]):
        out_ref[copy, 0:rows, :] = total
        out_ref[copy, rows : rows + own, :] = basis


def rank_of(row, core):
    return ((row >> 3) & 7) * 32 + (row >> 6) * 8 + core * 4 + (row & 3)


def project(scale, own, gathered_ref, grad_ref, out_ref):
    core = lax.axis_index("core")
    core = core if own else 1 - core
    width = out_ref.shape[1]
    chunk = gathered_ref.shape[0] // 8
    tokens = chunk - 16
    coefficients = jnp.concatenate(
        [gathered_ref[t * chunk : t * chunk + tokens, :] for t in range(8)], axis=0
    )
    rank = coefficients.shape[1]
    rows = out_ref.shape[0]
    place = one_hot(rank_of(iota((rows, rank), 0), core) == iota((rows, rank), 1))
    arranged = lax.dot_general(
        place, coefficients, (((1,), (1,)), ((), ())), preferred_element_type=F32
    ).astype(BF16)
    tile = 256
    first_half = (iota((rows, tile), 0) & 4) == 0
    for start in range(0, width, tile):
        low = jnp.dot(
            arranged, grad_ref[:, start : start + tile], preferred_element_type=F32
        )
        high = jnp.dot(
            arranged,
            grad_ref[:, width + start : width + start + tile],
            preferred_element_type=F32,
        )
        out_ref[:, start : start + tile] = (
            jnp.where(first_half, low, high) * scale
        ).astype(out_ref.dtype)


def add_halves(mine_ref, theirs_ref, out_ref):
    out_ref[...] = (mine_ref[...] + theirs_ref[...].astype(F32)).astype(BF16)


def adam(parts_ref, first_ref, second_ref, first_out_ref, second_out_ref, out_ref):
    rows, width = 4, parts_ref.shape[1]
    total = parts_ref[0:16, :].astype(F32)
    for part in range(1, parts_ref.shape[0] // 16):
        total += parts_ref[part * 16 : (part + 1) * 16, :].astype(F32)
    total = total[0:8, :] + total[8:16, :]
    directions = []
    for half in range(2):
        grad = total[half * rows : (half + 1) * rows, :]
        columns = slice(half * width, (half + 1) * width)
        first_out = BETA_ONE * first_ref[:, columns] + (1.0 - BETA_ONE) * grad
        second_out = BETA_TWO * second_ref[:, columns] + (1.0 - BETA_TWO) * grad * grad
        first_out_ref[:, columns] = first_out
        second_out_ref[:, columns] = second_out
        corrected = first_out / (1.0 - BETA_ONE**STEP)
        scaled = jnp.sqrt(second_out / (1.0 - BETA_TWO**STEP)) + EPS
        directions.append(corrected / scaled)
    block = jnp.concatenate(directions + directions, axis=0).astype(BF16)
    for part in range(out_ref.shape[0] // 16):
        out_ref[part * 16 : (part + 1) * 16, :] = block


def arrange_basis(gathered_ref, out_ref):
    core = lax.axis_index("core")
    chunk = gathered_ref.shape[0] // 8
    basis = jnp.concatenate(
        [gathered_ref[t * chunk + chunk - 16 : (t + 1) * chunk, :] for t in range(8)], axis=0
    )
    rank = basis.shape[1]
    r, place = iota((rank, rank), 0), iota((rank, rank), 1)
    for which in range(CORE):
        side = core if which == 0 else 1 - core
        for half in range(2):
            move = one_hot((r == rank_of(place, side)) & (((place >> 2) & 1) == half))
            out_ref[2 * which + half] = jnp.dot(
                basis, move, preferred_element_type=F32
            ).astype(BF16)


def expand_own(basis_ref, directions_ref, out_ref):
    width = directions_ref.shape[1]
    tile = 256
    for half in range(2):
        basis = basis_ref[half]
        for start in range(0, width, tile):
            out_ref[:, half * width + start : half * width + start + tile] = jnp.dot(
                basis, directions_ref[:, start : start + tile], preferred_element_type=F32
            )


def expand(basis_ref, part_ref, directions_ref, out_ref):
    width = directions_ref.shape[1]
    tile = 256
    for half in range(2):
        basis = basis_ref[2 + half]
        for start in range(0, width, tile):
            columns = slice(half * width + start, half * width + start + tile)
            out_ref[:, columns] = (
                part_ref[:, columns]
                + jnp.dot(
                    basis, directions_ref[:, start : start + tile], preferred_element_type=F32
                )
            ).astype(BF16)


def per_device(tokens, grad_gate, basis, first_moment, second_moment):
    rows, features = tokens.shape
    own, rank = basis.shape
    group_tokens, columns = grad_gate.shape
    half = columns // 2
    scale = 1.0 / math.sqrt(group_tokens * Z * Y_LO * CORE)
    shape = jax.ShapeDtypeStruct
    swap = [(0, 1), (1, 0)]

    def exchange(array, axes):
        return lax.all_to_all(array, axes, 0, 0, tiled=True)

    copies = Z * Y_LO * Y_HI
    basis_copies = jnp.broadcast_to(basis[None], (copies, own, rank))
    class_basis = exchange(basis_copies, ("z", "y_lo", "y_hi")).reshape(copies * own, rank)
    block = shape((rows, features // X), BF16)
    blocks = call(split_features, (block,) * X, 2 * rows * features * 512, 0)(tokens)
    held = [blocks[0]] + [
        lax.ppermute(blocks[step], "x", [(x, (x + step) % X) for x in range(X)])
        for step in range(1, X)
    ]
    stacked = call(
        stack, shape((X * rows, features // X), BF16), rows * features, 4 * rows * features
    )(*held)
    class_basis, stacked = lax.optimization_barrier((class_basis, stacked))
    sibling_basis = lax.ppermute(class_basis, "core", swap)
    part_shape = shape((X, rows, rank), F32)
    part_cost = (rows * features * rank, rows * features + copies * own * rank)
    part = call(partial_coefficients, part_shape, *part_cost)(class_basis, stacked)
    parts = call(whole_coefficients, part_shape, *part_cost)(
        sibling_basis, part, stacked
    )
    parts = exchange(parts, "x")
    takers = Y_HI * X
    chunk = rows + own
    gathered = exchange(
        call(
            sum_coefficients,
            shape((takers, chunk, rank), BF16),
            X * rows * rank,
            4 * takers * chunk * rank,
        )(parts, basis),
        ("y_hi", "x"),
    ).reshape(takers * chunk, rank)

    def projected(own_half, dtype):
        return call(
            functools.partial(project, scale, own_half),
            shape((rank, half), dtype),
            2 * rank * group_tokens * columns,
            2 * group_tokens * columns + 2 * rank * columns,
            )(gathered, grad_gate)

    theirs = lax.ppermute(projected(False, BF16), "core", swap)
    mine = projected(True, F32)
    pair = call(add_halves, shape((rank, half), BF16), rank * half, 8 * rank * half)(mine, theirs)
    owned = exchange(pair, ("y_lo", "z"))
    first_out, second_out, direction = call(
        adam,
        (
            shape(first_moment.shape, F32),
            shape(second_moment.shape, F32),
            shape((rank, half), BF16),
        ),
        rank * half,
        4 * rank * half,
    )(owned, first_moment, second_moment)
    directions = exchange(direction, ("y_lo", "z"))
    others = lax.ppermute(directions, "core", swap)
    update_rows = own * takers
    bases = call(
        arrange_basis, shape((4, update_rows, rank), BF16), 8 * update_rows * rank * rank, 0
    )(gathered)
    cost = (4 * update_rows * rank * half, 4 * update_rows * columns)
    part = call(expand_own, shape((update_rows, columns), F32), *cost)(bases, directions)
    update = call(expand, shape((update_rows, columns), BF16), *cost)(bases, part, others)
    return (update, first_out, second_out)


def solution(mesh):
    names = ("z", "y_lo", "core", "y_hi", "x")
    fine = Mesh(mesh.devices.reshape(Z, Y_LO, CORE, Y_HI, X), names)
    data, tensor = names[:3], names[3:]
    placed = (P(names, None), P(data, tensor), P(names, None), P(data, tensor), P(data, tensor))
    return jax.shard_map(
        per_device,
        mesh=fine,
        in_specs=placed,
        out_specs=(P(data, tensor), P(data, tensor), P(data, tensor)),
        check_vma=False,
    )
```

```python
import functools
import math

import jax
import jax.numpy as jnp
from jax import lax
from jax.experimental import pallas as pl
from jax.experimental.pallas import tpu as pltpu
from jax.sharding import Mesh
from jax.sharding import PartitionSpec as P

STEP = 10


BETA_ONE = 0.9
BETA_TWO = 0.95
EPS = 1e-08

Z_HI, Z_LO = 4, 2
Z, Y_LO, CORE, Y_HI, X = 8, 4, 2, 2, 4
OWNERS = Z * Y_LO
VMEM_LIMIT = 24 * 1024 * 1024
F32, BF16 = jnp.float32, jnp.bfloat16


def call(body, out_shape, flops, moved):
    return pl.pallas_call(
        body,
        out_shape=out_shape,
        compiler_params=pltpu.CompilerParams(vmem_limit_bytes=VMEM_LIMIT),
        cost_estimate=pl.CostEstimate(flops=flops, bytes_accessed=moved, transcendentals=0),
    )


def iota(shape, axis):
    return lax.broadcasted_iota(jnp.int32, shape, axis)


def one_hot(condition):
    return jnp.where(condition, 1.0, 0.0).astype(BF16)


def split_features(tokens_ref, *out_refs):
    here = lax.axis_index("x")
    width = Y_LO * 128
    p, q = iota((width, width), 0), iota((width, width), 1)
    steps = (((p >> 4) & 3) - here) & 3
    move = one_hot(steps * 128 + (p >> 7) * 32 + ((p >> 6) & 1) * 16 + (p & 15) == q)
    for z in range(Z):
        for side in range(CORE):
            block = jnp.concatenate(
                [
                    tokens_ref[:, pl.ds(((z * Y_LO + y) * CORE + side) * 128, 128)]
                    for y in range(Y_LO)
                ],
                axis=1,
            )
            moved = jnp.dot(block, move, preferred_element_type=F32).astype(BF16)
            start = (side * Z + z) * 128
            for x in range(X):
                out_refs[x][:, start : start + 128] = moved[:, x * 128 : (x + 1) * 128]


def stack(*refs):
    *block_refs, out_ref = refs
    rows = block_refs[0].shape[0]
    for step, ref in enumerate(block_refs):
        out_ref[step * rows : (step + 1) * rows, :] = ref[...]


def class_part(tokens_ref, basis_ref, side):
    width = basis_ref.shape[0]
    columns = pl.ds(pl.multiple_of(side * width, 128), width)
    return jnp.dot(tokens_ref[:, columns], basis_ref[...], preferred_element_type=F32)


def partial_coefficients(basis_ref, tokens_ref, out_ref):
    here, rows = lax.axis_index("x"), out_ref.shape[1]
    parts = class_part(tokens_ref, basis_ref, lax.axis_index("core"))
    for step in range(X):
        out_ref[(here - step) & 3] = parts[step * rows : (step + 1) * rows, :]


def whole_coefficients(basis_ref, part_ref, tokens_ref, out_ref):
    here, rows = lax.axis_index("x"), out_ref.shape[1]
    parts = class_part(tokens_ref, basis_ref, 1 - lax.axis_index("core"))
    for step in range(X):
        place = (here - step) & 3
        out_ref[place] = part_ref[place] + parts[step * rows : (step + 1) * rows, :]


def sum_coefficients(parts_ref, basis_ref, out_ref):
    rows = parts_ref.shape[1]
    own = basis_ref.shape[0]
    total = (parts_ref[0] + parts_ref[1]) + (parts_ref[2] + parts_ref[3])
    total = total.astype(BF16)
    basis = basis_ref[...]
    for copy in range(out_ref.shape[0]):
        out_ref[copy, 0:rows, :] = total
        out_ref[copy, rows : rows + own, :] = basis


def rank_of(row, core):
    return (row >> 3) * 8 + core * 4 + (row & 3)


def project(scale, own, gathered_ref, grad_ref, out_ref):
    core = lax.axis_index("core")
    core = core if own else 1 - core
    width = out_ref.shape[1]
    chunk = gathered_ref.shape[0] // 8
    tokens = chunk - 16
    coefficients = jnp.concatenate(
        [gathered_ref[t * chunk : t * chunk + tokens, :] for t in range(8)], axis=0
    )
    rank = coefficients.shape[1]
    rows = out_ref.shape[0]
    place = one_hot(rank_of(iota((rows, rank), 0), core) == iota((rows, rank), 1))
    arranged = lax.dot_general(
        place, coefficients, (((1,), (1,)), ((), ())), preferred_element_type=F32
    ).astype(BF16)
    tile = 256
    first_half = (iota((rows, tile), 0) & 4) == 0
    for start in range(0, width, tile):
        low = jnp.dot(
            arranged, grad_ref[:, start : start + tile], preferred_element_type=F32
        )
        high = jnp.dot(
            arranged,
            grad_ref[:, width + start : width + start + tile],
            preferred_element_type=F32,
        )
        out_ref[:, start : start + tile] = (
            jnp.where(first_half, low, high) * scale
        ).astype(out_ref.dtype)


def add_halves(mine_ref, theirs_ref, out_ref):
    out_ref[...] = (mine_ref[...] + theirs_ref[...].astype(F32)).astype(BF16)


def adam(parts_ref, first_ref, second_ref, first_out_ref, second_out_ref, out_ref):
    rows, width = 4, parts_ref.shape[1]
    total = parts_ref[0:16, :].astype(F32)
    for part in range(1, parts_ref.shape[0] // 16):
        total += parts_ref[part * 16 : (part + 1) * 16, :].astype(F32)
    total = total[0:8, :] + total[8:16, :]
    directions = []
    for half in range(2):
        grad = total[half * rows : (half + 1) * rows, :]
        columns = slice(half * width, (half + 1) * width)
        first_out = BETA_ONE * first_ref[:, columns] + (1.0 - BETA_ONE) * grad
        second_out = BETA_TWO * second_ref[:, columns] + (1.0 - BETA_TWO) * grad * grad
        first_out_ref[:, columns] = first_out
        second_out_ref[:, columns] = second_out
        corrected = first_out / (1.0 - BETA_ONE**STEP)
        scaled = jnp.sqrt(second_out / (1.0 - BETA_TWO**STEP)) + EPS
        directions.append(corrected / scaled)
    block = jnp.concatenate(directions + directions, axis=0).astype(BF16)
    for part in range(out_ref.shape[0] // 16):
        out_ref[part * 16 : (part + 1) * 16, :] = block


def arrange_basis(gathered_ref, out_ref):
    core, parity = lax.axis_index("core"), lax.axis_index("z_lo")
    chunk = gathered_ref.shape[0] // 8
    basis = jnp.concatenate(
        [gathered_ref[t * chunk + chunk - 16 : (t + 1) * chunk, :] for t in range(8)], axis=0
    )
    rank = basis.shape[1]
    r, place = iota((rank, rank), 0), iota((rank, rank), 1)
    side = jnp.where(place < rank // 2, core, 1 - core)
    owner = (place & (rank // 2 - 1)) >> 3
    for which in range(Z_LO):
        z = (owner >> 2) * 2 + (parity if which == 0 else 1 - parity)
        held = (z * Y_LO + (owner & 3)) * 8 + side * 4 + (place & 3)
        for half in range(2):
            move = one_hot((r == held) & (((place >> 2) & 1) == half))
            out_ref[2 * which + half] = jnp.dot(
                basis, move, preferred_element_type=F32
            ).astype(BF16)


def expand_own(basis_ref, own_ref, sibling_ref, out_ref):
    width = own_ref.shape[1]
    tile = 256
    for start in range(0, width, tile):
        columns = slice(start, start + tile)
        directions = jnp.concatenate([own_ref[:, columns], sibling_ref[:, columns]], axis=0)
        for half in range(2):
            out_ref[:, half * width + start : half * width + start + tile] = jnp.dot(
                basis_ref[half], directions, preferred_element_type=F32
            )


def expand(basis_ref, part_ref, *refs):
    *block_refs, out_ref = refs
    width = block_refs[0].shape[1]
    tile = 256
    for start in range(0, width, tile):
        columns = slice(start, start + tile)
        directions = jnp.concatenate([ref[:, columns] for ref in block_refs], axis=0)
        for half in range(2):
            there = slice(half * width + start, half * width + start + tile)
            out_ref[:, there] = (
                part_ref[:, there]
                + jnp.dot(basis_ref[2 + half], directions, preferred_element_type=F32)
            ).astype(BF16)


def per_device(tokens, grad_gate, basis, first_moment, second_moment):
    rows, features = tokens.shape
    own, rank = basis.shape
    group_tokens, columns = grad_gate.shape
    half = columns // 2
    scale = 1.0 / math.sqrt(group_tokens * Z * Y_LO * CORE)
    shape = jax.ShapeDtypeStruct
    swap = [(0, 1), (1, 0)]

    def exchange(array, axes):
        return lax.all_to_all(array, axes, 0, 0, tiled=True)

    copies = Z * Y_LO * Y_HI
    basis_copies = jnp.broadcast_to(basis[None], (copies, own, rank))
    class_basis = exchange(basis_copies, ("z_hi", "z_lo", "y_lo", "y_hi")).reshape(copies * own, rank)
    block = shape((rows, features // X), BF16)
    blocks = call(split_features, (block,) * X, 2 * rows * features * 512, 0)(tokens)
    held = [blocks[0]] + [
        lax.ppermute(blocks[step], "x", [(x, (x + step) % X) for x in range(X)])
        for step in range(1, X)
    ]
    stacked = call(
        stack, shape((X * rows, features // X), BF16), rows * features, 4 * rows * features
    )(*held)
    class_basis, stacked = lax.optimization_barrier((class_basis, stacked))
    sibling_basis = lax.ppermute(class_basis, "core", swap)
    part_shape = shape((X, rows, rank), F32)
    part_cost = (rows * features * rank, rows * features + copies * own * rank)
    part = call(partial_coefficients, part_shape, *part_cost)(class_basis, stacked)
    parts = call(whole_coefficients, part_shape, *part_cost)(
        sibling_basis, part, stacked
    )
    parts = exchange(parts, "x")
    takers = Y_HI * X
    chunk = rows + own
    gathered = exchange(
        call(
            sum_coefficients,
            shape((takers, chunk, rank), BF16),
            X * rows * rank,
            4 * takers * chunk * rank,
        )(parts, basis),
        ("y_hi", "x"),
    ).reshape(takers * chunk, rank)

    def projected(own_half, dtype):
        return call(
            functools.partial(project, scale, own_half),
            shape((rank, half), dtype),
            2 * rank * group_tokens * columns,
            2 * group_tokens * columns + 2 * rank * columns,
            )(gathered, grad_gate)

    theirs = lax.ppermute(projected(False, BF16), "core", swap)
    mine = projected(True, F32)
    pair = call(add_halves, shape((rank, half), BF16), rank * half, 8 * rank * half)(mine, theirs)
    owned = exchange(pair, ("z_hi", "z_lo", "y_lo"))
    first_out, second_out, direction = call(
        adam,
        (
            shape(first_moment.shape, F32),
            shape(second_moment.shape, F32),
            shape((rank // Z_LO, half), BF16),
        ),
        rank * half,
        4 * rank * half,
    )(owned, first_moment, second_moment)
    same = exchange(direction, ("z_hi", "y_lo"))
    middle = same.shape[0] // 2

    def along_z(array, step):
        return lax.ppermute(array, ("z_hi", "z_lo"), [(z, (z + step) % Z) for z in range(Z)])

    upper, lower = along_z(same[:middle], 1), along_z(same[middle:], -1)
    sibling_same = lax.ppermute(same, "core", swap)
    sibling_upper = lax.ppermute(upper, "core", swap)
    sibling_lower = lax.ppermute(lower, "core", swap)
    update_rows = own * takers
    bases = call(
        arrange_basis, shape((4, update_rows, rank), BF16), 8 * update_rows * rank * rank, 0
    )(gathered)
    cost = (4 * update_rows * rank * half, 4 * update_rows * columns)
    part = call(expand_own, shape((update_rows, columns), F32), *cost)(bases, same, sibling_same)
    update = call(expand, shape((update_rows, columns), BF16), *cost)(
        bases, part, upper, lower, sibling_upper, sibling_lower
    )
    return (update, first_out, second_out)


def solution(mesh):
    names = ("z_hi", "z_lo", "y_lo", "core", "y_hi", "x")
    fine = Mesh(mesh.devices.reshape(Z_HI, Z_LO, Y_LO, CORE, Y_HI, X), names)
    data, tensor = names[:4], names[4:]
    placed = (P(names, None), P(data, tensor), P(names, None), P(data, tensor), P(data, tensor))
    return jax.shard_map(
        per_device,
        mesh=fine,
        in_specs=placed,
        out_specs=(P(data, tensor), P(data, tensor), P(data, tensor)),
        check_vma=False,
    )
```

```python
import functools
import math

import jax
import jax.numpy as jnp
from jax import lax
from jax.experimental import pallas as pl
from jax.experimental.pallas import tpu as pltpu
from jax.sharding import Mesh
from jax.sharding import PartitionSpec as P

STEP = 10


BETA_ONE = 0.9
BETA_TWO = 0.95
EPS = 1e-08

Z_HI, Z_LO = 4, 2
Z, Y_LO, CORE, Y_HI, X = 8, 4, 2, 2, 4
OWNERS = Z * Y_LO
VMEM_LIMIT = 24 * 1024 * 1024
F32, BF16 = jnp.float32, jnp.bfloat16


def call(body, out_shape, flops, moved):
    return pl.pallas_call(
        body,
        out_shape=out_shape,
        compiler_params=pltpu.CompilerParams(vmem_limit_bytes=VMEM_LIMIT),
        cost_estimate=pl.CostEstimate(flops=flops, bytes_accessed=moved, transcendentals=0),
    )


def iota(shape, axis):
    return lax.broadcasted_iota(jnp.int32, shape, axis)


def one_hot(condition):
    return jnp.where(condition, 1.0, 0.0).astype(BF16)


def split_features(tokens_ref, *out_refs):
    here = lax.axis_index("x")
    width = Y_LO * 128
    p, q = iota((width, width), 0), iota((width, width), 1)
    steps = (((p >> 4) & 3) - here) & 3
    move = one_hot(steps * 128 + (p >> 7) * 32 + ((p >> 6) & 1) * 16 + (p & 15) == q)
    for z in range(Z):
        for side in range(CORE):
            block = jnp.concatenate(
                [
                    tokens_ref[:, pl.ds(((z * Y_LO + y) * CORE + side) * 128, 128)]
                    for y in range(Y_LO)
                ],
                axis=1,
            )
            moved = jnp.dot(block, move, preferred_element_type=F32).astype(BF16)
            start = (side * Z + z) * 128
            for x in range(X):
                out_refs[x][:, start : start + 128] = moved[:, x * 128 : (x + 1) * 128]


def stack(*refs):
    *block_refs, out_ref = refs
    start = 0
    for ref in block_refs:
        rows = ref.shape[0]
        out_ref[start : start + rows, :] = ref[...]
        start += rows


def class_part(tokens_ref, basis_ref, side):
    width = basis_ref.shape[0]
    columns = pl.ds(pl.multiple_of(side * width, 128), width)
    return jnp.dot(tokens_ref[:, columns], basis_ref[...], preferred_element_type=F32)


def partial_coefficients(basis_ref, tokens_ref, out_ref):
    here, rows = lax.axis_index("x"), out_ref.shape[1]
    parts = class_part(tokens_ref, basis_ref, lax.axis_index("core"))
    for step in range(X):
        out_ref[(here - step) & 3] = parts[step * rows : (step + 1) * rows, :]


def whole_coefficients(basis_ref, part_ref, tokens_ref, out_ref):
    here, rows = lax.axis_index("x"), out_ref.shape[1]
    parts = class_part(tokens_ref, basis_ref, 1 - lax.axis_index("core"))
    for step in range(X):
        place = (here - step) & 3
        out_ref[place] = part_ref[place] + parts[step * rows : (step + 1) * rows, :]


def sum_coefficients(parts_ref, basis_ref, out_ref):
    rows = parts_ref.shape[1]
    own = basis_ref.shape[0]
    total = (parts_ref[0] + parts_ref[1]) + (parts_ref[2] + parts_ref[3])
    total = total.astype(BF16)
    basis = basis_ref[...]
    for copy in range(out_ref.shape[0]):
        out_ref[copy, 0:rows, :] = total
        out_ref[copy, rows : rows + own, :] = basis


def rank_of(row, core):
    return (row >> 3) * 8 + core * 4 + (row & 3)


def project(scale, own, gathered_ref, grad_ref, out_ref):
    core = lax.axis_index("core")
    core = core if own else 1 - core
    width = out_ref.shape[1]
    chunk = gathered_ref.shape[0] // 8
    tokens = chunk - 16
    coefficients = jnp.concatenate(
        [gathered_ref[t * chunk : t * chunk + tokens, :] for t in range(8)], axis=0
    )
    rank = coefficients.shape[1]
    rows = out_ref.shape[0]
    place = one_hot(rank_of(iota((rows, rank), 0), core) == iota((rows, rank), 1))
    arranged = lax.dot_general(
        place, coefficients, (((1,), (1,)), ((), ())), preferred_element_type=F32
    ).astype(BF16)
    tile = 256
    first_half = (iota((rows, tile), 0) & 4) == 0
    for start in range(0, width, tile):
        low = jnp.dot(
            arranged, grad_ref[:, start : start + tile], preferred_element_type=F32
        )
        high = jnp.dot(
            arranged,
            grad_ref[:, width + start : width + start + tile],
            preferred_element_type=F32,
        )
        out_ref[:, start : start + tile] = (
            jnp.where(first_half, low, high) * scale
        ).astype(out_ref.dtype)


def add_halves(mine_ref, theirs_ref, out_ref):
    out_ref[...] = (mine_ref[...] + theirs_ref[...].astype(F32)).astype(BF16)


def adam(parts_ref, first_ref, second_ref, first_out_ref, second_out_ref, out_ref):
    rows, width = 4, parts_ref.shape[1]
    total = parts_ref[0:16, :].astype(F32)
    for part in range(1, parts_ref.shape[0] // 16):
        total += parts_ref[part * 16 : (part + 1) * 16, :].astype(F32)
    total = total[0:8, :] + total[8:16, :]
    directions = []
    for half in range(2):
        grad = total[half * rows : (half + 1) * rows, :]
        columns = slice(half * width, (half + 1) * width)
        first_out = BETA_ONE * first_ref[:, columns] + (1.0 - BETA_ONE) * grad
        second_out = BETA_TWO * second_ref[:, columns] + (1.0 - BETA_TWO) * grad * grad
        first_out_ref[:, columns] = first_out
        second_out_ref[:, columns] = second_out
        corrected = first_out / (1.0 - BETA_ONE**STEP)
        scaled = jnp.sqrt(second_out / (1.0 - BETA_TWO**STEP)) + EPS
        directions.append(corrected / scaled)
    block = jnp.concatenate(directions + directions, axis=0).astype(BF16)
    for part in range(out_ref.shape[0] // 16):
        out_ref[part * 16 : (part + 1) * 16, :] = block


def arrange_basis(gathered_ref, out_ref):
    core, parity = lax.axis_index("core"), lax.axis_index("z_lo")
    chunk = gathered_ref.shape[0] // 8
    basis = jnp.concatenate(
        [gathered_ref[t * chunk + chunk - 16 : (t + 1) * chunk, :] for t in range(8)], axis=0
    )
    rank = basis.shape[1]
    r, place = iota((rank, rank), 0), iota((rank, rank), 1)
    owner = (place & (rank // 2 - 1)) >> 3
    z = (owner >> 2) * 2 + jnp.where(place < rank // 2, parity, 1 - parity)
    for which in range(CORE):
        side = core if which == 0 else 1 - core
        held = (z * Y_LO + (owner & 3)) * 8 + side * 4 + (place & 3)
        for half in range(2):
            move = one_hot((r == held) & (((place >> 2) & 1) == half))
            out_ref[2 * which + half] = jnp.dot(
                basis, move, preferred_element_type=F32
            ).astype(BF16)


def expand_own(basis_ref, directions_ref, out_ref):
    width = directions_ref.shape[1]
    tile = 256
    for half in range(2):
        basis = basis_ref[half]
        for start in range(0, width, tile):
            out_ref[:, half * width + start : half * width + start + tile] = jnp.dot(
                basis, directions_ref[:, start : start + tile], preferred_element_type=F32
            )


def expand(basis_ref, part_ref, directions_ref, out_ref):
    width = directions_ref.shape[1]
    tile = 256
    for half in range(2):
        basis = basis_ref[2 + half]
        for start in range(0, width, tile):
            columns = slice(half * width + start, half * width + start + tile)
            out_ref[:, columns] = (
                part_ref[:, columns]
                + jnp.dot(
                    basis, directions_ref[:, start : start + tile], preferred_element_type=F32
                )
            ).astype(BF16)


def per_device(tokens, grad_gate, basis, first_moment, second_moment):
    rows, features = tokens.shape
    own, rank = basis.shape
    group_tokens, columns = grad_gate.shape
    half = columns // 2
    scale = 1.0 / math.sqrt(group_tokens * Z * Y_LO * CORE)
    shape = jax.ShapeDtypeStruct
    swap = [(0, 1), (1, 0)]

    def exchange(array, axes):
        return lax.all_to_all(array, axes, 0, 0, tiled=True)

    copies = Z * Y_LO * Y_HI
    basis_copies = jnp.broadcast_to(basis[None], (copies, own, rank))
    class_basis = exchange(basis_copies, ("z_hi", "z_lo", "y_lo", "y_hi")).reshape(copies * own, rank)
    block = shape((rows, features // X), BF16)
    blocks = call(split_features, (block,) * X, 2 * rows * features * 512, 0)(tokens)
    held = [blocks[0]] + [
        lax.ppermute(blocks[step], "x", [(x, (x + step) % X) for x in range(X)])
        for step in range(1, X)
    ]
    stacked = call(
        stack, shape((X * rows, features // X), BF16), rows * features, 4 * rows * features
    )(*held)
    class_basis, stacked = lax.optimization_barrier((class_basis, stacked))
    sibling_basis = lax.ppermute(class_basis, "core", swap)
    part_shape = shape((X, rows, rank), F32)
    part_cost = (rows * features * rank, rows * features + copies * own * rank)
    part = call(partial_coefficients, part_shape, *part_cost)(class_basis, stacked)
    parts = call(whole_coefficients, part_shape, *part_cost)(
        sibling_basis, part, stacked
    )
    parts = exchange(parts, "x")
    takers = Y_HI * X
    chunk = rows + own
    gathered = exchange(
        call(
            sum_coefficients,
            shape((takers, chunk, rank), BF16),
            X * rows * rank,
            4 * takers * chunk * rank,
        )(parts, basis),
        ("y_hi", "x"),
    ).reshape(takers * chunk, rank)

    def projected(own_half, dtype):
        return call(
            functools.partial(project, scale, own_half),
            shape((rank, half), dtype),
            2 * rank * group_tokens * columns,
            2 * group_tokens * columns + 2 * rank * columns,
            )(gathered, grad_gate)

    theirs = lax.ppermute(projected(False, BF16), "core", swap)
    mine = projected(True, F32)
    pair = call(add_halves, shape((rank, half), BF16), rank * half, 8 * rank * half)(mine, theirs)
    owned = exchange(pair, ("z_hi", "z_lo", "y_lo"))
    first_out, second_out, direction = call(
        adam,
        (
            shape(first_moment.shape, F32),
            shape(second_moment.shape, F32),
            shape((rank // Z_LO, half), BF16),
        ),
        rank * half,
        4 * rank * half,
    )(owned, first_moment, second_moment)
    same = exchange(direction, ("z_hi", "y_lo"))
    middle = same.shape[0] // 2

    def along_z(array, step):
        return lax.ppermute(array, ("z_hi", "z_lo"), [(z, (z + step) % Z) for z in range(Z)])

    upper, lower = along_z(same[:middle], 1), along_z(same[middle:], -1)
    directions = call(stack, shape((rank, half), BF16), 0, 4 * rank * half)(same, upper, lower)
    others = lax.ppermute(directions, "core", swap)
    update_rows = own * takers
    bases = call(
        arrange_basis, shape((4, update_rows, rank), BF16), 8 * update_rows * rank * rank, 0
    )(gathered)
    cost = (4 * update_rows * rank * half, 4 * update_rows * columns)
    part = call(expand_own, shape((update_rows, columns), F32), *cost)(bases, directions)
    update = call(expand, shape((update_rows, columns), BF16), *cost)(bases, part, others)
    return (update, first_out, second_out)


def solution(mesh):
    names = ("z_hi", "z_lo", "y_lo", "core", "y_hi", "x")
    fine = Mesh(mesh.devices.reshape(Z_HI, Z_LO, Y_LO, CORE, Y_HI, X), names)
    data, tensor = names[:4], names[4:]
    placed = (P(names, None), P(data, tensor), P(names, None), P(data, tensor), P(data, tensor))
    return jax.shard_map(
        per_device,
        mesh=fine,
        in_specs=placed,
        out_specs=(P(data, tensor), P(data, tensor), P(data, tensor)),
        check_vma=False,
    )
```

```python
import functools
import math

import jax
import jax.numpy as jnp
from jax import lax
from jax.experimental import pallas as pl
from jax.experimental.pallas import tpu as pltpu
from jax.sharding import Mesh
from jax.sharding import PartitionSpec as P

STEP = 10


BETA_ONE = 0.9
BETA_TWO = 0.95
EPS = 1e-08

Z, Y_LO, CORE, Y_HI, X = 8, 4, 2, 2, 4
OWNERS = Z * Y_LO
VMEM_LIMIT = 24 * 1024 * 1024
F32, BF16 = jnp.float32, jnp.bfloat16


def call(body, out_shape, flops, moved):
    return pl.pallas_call(
        body,
        out_shape=out_shape,
        compiler_params=pltpu.CompilerParams(vmem_limit_bytes=VMEM_LIMIT),
        cost_estimate=pl.CostEstimate(flops=flops, bytes_accessed=moved, transcendentals=0),
    )


def iota(shape, axis):
    return lax.broadcasted_iota(jnp.int32, shape, axis)


def one_hot(condition):
    return jnp.where(condition, 1.0, 0.0).astype(BF16)


def split_features(tokens_ref, *out_refs):
    here = lax.axis_index("x")
    width = Y_LO * 128
    p, q = iota((width, width), 0), iota((width, width), 1)
    steps = (((p >> 4) & 3) - here) & 3
    move = one_hot(steps * 128 + (p >> 7) * 32 + ((p >> 6) & 1) * 16 + (p & 15) == q)
    for z in range(Z):
        for side in range(CORE):
            block = jnp.concatenate(
                [
                    tokens_ref[:, pl.ds(((z * Y_LO + y) * CORE + side) * 128, 128)]
                    for y in range(Y_LO)
                ],
                axis=1,
            )
            moved = jnp.dot(block, move, preferred_element_type=F32).astype(BF16)
            start = (side * Z + z) * 128
            for x in range(X):
                out_refs[x][:, start : start + 128] = moved[:, x * 128 : (x + 1) * 128]


def stack(*refs):
    *block_refs, out_ref = refs
    rows = block_refs[0].shape[0]
    for step, ref in enumerate(block_refs):
        out_ref[step * rows : (step + 1) * rows, :] = ref[...]


def class_part(tokens_ref, basis_ref, side):
    width = basis_ref.shape[0]
    columns = pl.ds(pl.multiple_of(side * width, 128), width)
    return jnp.dot(tokens_ref[:, columns], basis_ref[...], preferred_element_type=F32)


def partial_coefficients(basis_ref, tokens_ref, out_ref):
    here, rows = lax.axis_index("x"), out_ref.shape[1]
    parts = class_part(tokens_ref, basis_ref, lax.axis_index("core"))
    for step in range(X):
        out_ref[(here - step) & 3] = parts[step * rows : (step + 1) * rows, :]


def whole_coefficients(basis_ref, part_ref, tokens_ref, out_ref):
    here, rows = lax.axis_index("x"), out_ref.shape[1]
    parts = class_part(tokens_ref, basis_ref, 1 - lax.axis_index("core"))
    for step in range(X):
        place = (here - step) & 3
        out_ref[place] = part_ref[place] + parts[step * rows : (step + 1) * rows, :]


def sum_coefficients(parts_ref, basis_ref, out_ref):
    rows = parts_ref.shape[1]
    own = basis_ref.shape[0]
    total = (parts_ref[0] + parts_ref[1]) + (parts_ref[2] + parts_ref[3])
    total = total.astype(BF16)
    basis = basis_ref[...]
    for copy in range(out_ref.shape[0]):
        out_ref[copy, 0:rows, :] = total
        out_ref[copy, rows : rows + own, :] = basis


def rank_of(row, core):
    return (row >> 3) * 8 + core * 4 + (row & 3)


def project(scale, own, gathered_ref, grad_ref, out_ref):
    core = lax.axis_index("core")
    core = core if own else 1 - core
    width = out_ref.shape[1]
    chunk = gathered_ref.shape[0] // 8
    tokens = chunk - 16
    coefficients = jnp.concatenate(
        [gathered_ref[t * chunk : t * chunk + tokens, :] for t in range(8)], axis=0
    )
    rank = coefficients.shape[1]
    rows = out_ref.shape[0]
    place = one_hot(rank_of(iota((rows, rank), 0), core) == iota((rows, rank), 1))
    arranged = lax.dot_general(
        place, coefficients, (((1,), (1,)), ((), ())), preferred_element_type=F32
    ).astype(BF16)
    tile = 896
    first_half = (iota((rows, tile), 0) & 4) == 0
    for start in range(0, width, tile):
        low = jnp.dot(
            arranged, grad_ref[:, start : start + tile], preferred_element_type=F32
        )
        high = jnp.dot(
            arranged,
            grad_ref[:, width + start : width + start + tile],
            preferred_element_type=F32,
        )
        out_ref[:, start : start + tile] = (
            jnp.where(first_half, low, high) * scale
        ).astype(out_ref.dtype)


def add_halves(mine_ref, theirs_ref, out_ref):
    out_ref[...] = (mine_ref[...] + theirs_ref[...].astype(F32)).astype(BF16)


def adam(parts_ref, first_ref, second_ref, first_out_ref, second_out_ref, out_ref):
    rows, width = 4, parts_ref.shape[1]
    total = parts_ref[0:16, :].astype(F32)
    for part in range(1, parts_ref.shape[0] // 16):
        total += parts_ref[part * 16 : (part + 1) * 16, :].astype(F32)
    total = total[0:8, :] + total[8:16, :]
    directions = []
    for half in range(2):
        grad = total[half * rows : (half + 1) * rows, :]
        columns = slice(half * width, (half + 1) * width)
        first_out = BETA_ONE * first_ref[:, columns] + (1.0 - BETA_ONE) * grad
        second_out = BETA_TWO * second_ref[:, columns] + (1.0 - BETA_TWO) * grad * grad
        first_out_ref[:, columns] = first_out
        second_out_ref[:, columns] = second_out
        corrected = first_out / (1.0 - BETA_ONE**STEP)
        scaled = jnp.sqrt(second_out / (1.0 - BETA_TWO**STEP)) + EPS
        directions.append(corrected / scaled)
    block = jnp.concatenate(directions + directions, axis=0).astype(BF16)
    for part in range(out_ref.shape[0] // 16):
        out_ref[part * 16 : (part + 1) * 16, :] = block


def arrange_basis(gathered_ref, out_ref):
    core = lax.axis_index("core")
    chunk = gathered_ref.shape[0] // 8
    basis = jnp.concatenate(
        [gathered_ref[t * chunk + chunk - 16 : (t + 1) * chunk, :] for t in range(8)], axis=0
    )
    rank = basis.shape[1]
    r, place = iota((rank, rank), 0), iota((rank, rank), 1)
    for which in range(CORE):
        side = core if which == 0 else 1 - core
        for half in range(2):
            move = one_hot((r == rank_of(place, side)) & (((place >> 2) & 1) == half))
            out_ref[2 * which + half] = jnp.dot(
                basis, move, preferred_element_type=F32
            ).astype(BF16)


def expand_own(basis_ref, directions_ref, out_ref):
    width = directions_ref.shape[1]
    tile = 896
    for half in range(2):
        basis = basis_ref[half]
        for start in range(0, width, tile):
            out_ref[:, half * width + start : half * width + start + tile] = jnp.dot(
                basis, directions_ref[:, start : start + tile], preferred_element_type=F32
            )


def expand(basis_ref, part_ref, directions_ref, out_ref):
    width = directions_ref.shape[1]
    tile = 896
    for half in range(2):
        basis = basis_ref[2 + half]
        for start in range(0, width, tile):
            columns = slice(half * width + start, half * width + start + tile)
            out_ref[:, columns] = (
                part_ref[:, columns]
                + jnp.dot(
                    basis, directions_ref[:, start : start + tile], preferred_element_type=F32
                )
            ).astype(BF16)


def per_device(tokens, grad_gate, basis, first_moment, second_moment):
    rows, features = tokens.shape
    own, rank = basis.shape
    group_tokens, columns = grad_gate.shape
    half = columns // 2
    scale = 1.0 / math.sqrt(group_tokens * Z * Y_LO * CORE)
    shape = jax.ShapeDtypeStruct
    swap = [(0, 1), (1, 0)]

    def exchange(array, axes):
        return lax.all_to_all(array, axes, 0, 0, tiled=True)

    copies = Z * Y_LO * Y_HI
    basis_copies = jnp.broadcast_to(basis[None], (copies, own, rank))
    class_basis = exchange(basis_copies, ("z", "y_lo", "y_hi")).reshape(copies * own, rank)
    block = shape((rows, features // X), BF16)
    blocks = call(split_features, (block,) * X, 2 * rows * features * 512, 0)(tokens)
    held = [blocks[0]] + [
        lax.ppermute(blocks[step], "x", [(x, (x + step) % X) for x in range(X)])
        for step in range(1, X)
    ]
    stacked = call(
        stack, shape((X * rows, features // X), BF16), rows * features, 4 * rows * features
    )(*held)
    class_basis, stacked = lax.optimization_barrier((class_basis, stacked))
    sibling_basis = lax.ppermute(class_basis, "core", swap)
    part_shape = shape((X, rows, rank), F32)
    part_cost = (rows * features * rank, rows * features + copies * own * rank)
    part = call(partial_coefficients, part_shape, *part_cost)(class_basis, stacked)
    parts = call(whole_coefficients, part_shape, *part_cost)(
        sibling_basis, part, stacked
    )
    parts = exchange(parts, "x")
    takers = Y_HI * X
    chunk = rows + own
    gathered = exchange(
        call(
            sum_coefficients,
            shape((takers, chunk, rank), BF16),
            X * rows * rank,
            4 * takers * chunk * rank,
        )(parts, basis),
        ("y_hi", "x"),
    ).reshape(takers * chunk, rank)

    def projected(own_half, dtype):
        return call(
            functools.partial(project, scale, own_half),
            shape((rank, half), dtype),
            2 * rank * group_tokens * columns,
            2 * group_tokens * columns + 2 * rank * columns,
            )(gathered, grad_gate)

    theirs = lax.ppermute(projected(False, BF16), "core", swap)
    mine = projected(True, F32)
    pair = call(add_halves, shape((rank, half), BF16), rank * half, 8 * rank * half)(mine, theirs)
    owned = exchange(pair, ("z", "y_lo"))
    first_out, second_out, direction = call(
        adam,
        (
            shape(first_moment.shape, F32),
            shape(second_moment.shape, F32),
            shape((rank, half), BF16),
        ),
        rank * half,
        4 * rank * half,
    )(owned, first_moment, second_moment)
    directions = exchange(direction, ("z", "y_lo"))
    others = lax.ppermute(directions, "core", swap)
    update_rows = own * takers
    bases = call(
        arrange_basis, shape((4, update_rows, rank), BF16), 8 * update_rows * rank * rank, 0
    )(gathered)
    cost = (4 * update_rows * rank * half, 4 * update_rows * columns)
    part = call(expand_own, shape((update_rows, columns), F32), *cost)(bases, directions)
    update = call(expand, shape((update_rows, columns), BF16), *cost)(bases, part, others)
    return (update, first_out, second_out)


def solution(mesh):
    names = ("z", "y_lo", "core", "y_hi", "x")
    fine = Mesh(mesh.devices.reshape(Z, Y_LO, CORE, Y_HI, X), names)
    data, tensor = names[:3], names[3:]
    placed = (P(names, None), P(data, tensor), P(names, None), P(data, tensor), P(data, tensor))
    return jax.shard_map(
        per_device,
        mesh=fine,
        in_specs=placed,
        out_specs=(P(data, tensor), P(data, tensor), P(data, tensor)),
        check_vma=False,
    )
```

```python
import functools
import math

import jax
import jax.numpy as jnp
from jax import lax
from jax.experimental import pallas as pl
from jax.experimental.pallas import tpu as pltpu
from jax.sharding import Mesh
from jax.sharding import PartitionSpec as P

STEP = 10


BETA_ONE = 0.9
BETA_TWO = 0.95
EPS = 1e-08

Z, Y_LO, CORE, Y_HI, X = 8, 4, 2, 2, 4
OWNERS = Z * Y_LO
VMEM_LIMIT = 24 * 1024 * 1024
F32, BF16 = jnp.float32, jnp.bfloat16


def call(body, out_shape, flops, moved):
    return pl.pallas_call(
        body,
        out_shape=out_shape,
        compiler_params=pltpu.CompilerParams(vmem_limit_bytes=VMEM_LIMIT),
        cost_estimate=pl.CostEstimate(flops=flops, bytes_accessed=moved, transcendentals=0),
    )


def iota(shape, axis):
    return lax.broadcasted_iota(jnp.int32, shape, axis)


def one_hot(condition):
    return jnp.where(condition, 1.0, 0.0).astype(BF16)


def split_features(tokens_ref, *out_refs):
    here = lax.axis_index("x")
    width = Y_LO * 128
    p, q = iota((width, width), 0), iota((width, width), 1)
    steps = (((p >> 4) & 3) - here) & 3
    move = one_hot(steps * 128 + (p >> 7) * 32 + ((p >> 6) & 1) * 16 + (p & 15) == q)
    for z in range(Z):
        for side in range(CORE):
            block = jnp.concatenate(
                [
                    tokens_ref[:, pl.ds(((z * Y_LO + y) * CORE + side) * 128, 128)]
                    for y in range(Y_LO)
                ],
                axis=1,
            )
            moved = jnp.dot(block, move, preferred_element_type=F32).astype(BF16)
            start = (side * Z + z) * 128
            for x in range(X):
                out_refs[x][:, start : start + 128] = moved[:, x * 128 : (x + 1) * 128]


def stack(*refs):
    *block_refs, out_ref = refs
    rows = block_refs[0].shape[0]
    for step, ref in enumerate(block_refs):
        out_ref[step * rows : (step + 1) * rows, :] = ref[...]


def class_part(tokens_ref, basis_ref, side):
    width = basis_ref.shape[0]
    columns = pl.ds(pl.multiple_of(side * width, 128), width)
    return jnp.dot(tokens_ref[:, columns], basis_ref[...], preferred_element_type=F32)


def partial_coefficients(basis_ref, tokens_ref, out_ref):
    here, rows = lax.axis_index("x"), out_ref.shape[1]
    parts = class_part(tokens_ref, basis_ref, lax.axis_index("core"))
    for step in range(X):
        out_ref[(here - step) & 3] = parts[step * rows : (step + 1) * rows, :]


def whole_coefficients(basis_ref, part_ref, tokens_ref, out_ref):
    here, rows = lax.axis_index("x"), out_ref.shape[1]
    parts = class_part(tokens_ref, basis_ref, 1 - lax.axis_index("core"))
    for step in range(X):
        place = (here - step) & 3
        out_ref[place] = part_ref[place] + parts[step * rows : (step + 1) * rows, :]


def sum_coefficients(parts_ref, basis_ref, out_ref):
    rows = parts_ref.shape[1]
    own = basis_ref.shape[0]
    total = (parts_ref[0] + parts_ref[1]) + (parts_ref[2] + parts_ref[3])
    total = total.astype(BF16)
    basis = basis_ref[...]
    for copy in range(out_ref.shape[0]):
        out_ref[copy, 0:rows, :] = total
        out_ref[copy, rows : rows + own, :] = basis


def rank_of(row, core):
    return (row >> 3) * 8 + core * 4 + (row & 3)


def project(scale, own, gathered_ref, grad_ref, out_ref):
    core = lax.axis_index("core")
    core = core if own else 1 - core
    width = out_ref.shape[1]
    chunk = gathered_ref.shape[0] // 8
    tokens = chunk - 16
    coefficients = jnp.concatenate(
        [gathered_ref[t * chunk : t * chunk + tokens, :] for t in range(8)], axis=0
    )
    rank = coefficients.shape[1]
    rows = out_ref.shape[0]
    place = one_hot(rank_of(iota((rows, rank), 0), core) == iota((rows, rank), 1))
    arranged = lax.dot_general(
        place, coefficients, (((1,), (1,)), ((), ())), preferred_element_type=F32
    ).astype(BF16)
    tile = 256
    first_half = (iota((rows, tile), 0) & 4) == 0
    for start in range(0, width, tile):
        low = jnp.dot(
            arranged, grad_ref[:, start : start + tile], preferred_element_type=F32
        )
        high = jnp.dot(
            arranged,
            grad_ref[:, width + start : width + start + tile],
            preferred_element_type=F32,
        )
        out_ref[:, start : start + tile] = (
            jnp.where(first_half, low, high) * scale
        ).astype(out_ref.dtype)


def add_halves(mine_ref, theirs_ref, out_ref):
    out_ref[...] = (mine_ref[...] + theirs_ref[...].astype(F32)).astype(BF16)


def adam(parts_ref, first_ref, second_ref, first_out_ref, second_out_ref, out_ref):
    rows, width = 4, parts_ref.shape[1]
    total = parts_ref[0:16, :].astype(F32)
    for part in range(1, parts_ref.shape[0] // 16):
        total += parts_ref[part * 16 : (part + 1) * 16, :].astype(F32)
    total = total[0:8, :] + total[8:16, :]
    directions = []
    for half in range(2):
        grad = total[half * rows : (half + 1) * rows, :]
        columns = slice(half * width, (half + 1) * width)
        first_out = BETA_ONE * first_ref[:, columns] + (1.0 - BETA_ONE) * grad
        second_out = BETA_TWO * second_ref[:, columns] + (1.0 - BETA_TWO) * grad * grad
        first_out_ref[:, columns] = first_out
        second_out_ref[:, columns] = second_out
        corrected = first_out / (1.0 - BETA_ONE**STEP)
        scaled = jnp.sqrt(second_out / (1.0 - BETA_TWO**STEP)) + EPS
        directions.append(corrected / scaled)
    block = jnp.concatenate(directions + directions, axis=0).astype(BF16)
    for part in range(out_ref.shape[0] // 16):
        out_ref[part * 16 : (part + 1) * 16, :] = block


def arrange_basis(gathered_ref, out_ref):
    core = lax.axis_index("core")
    chunk = gathered_ref.shape[0] // 8
    basis = jnp.concatenate(
        [gathered_ref[t * chunk + chunk - 16 : (t + 1) * chunk, :] for t in range(8)], axis=0
    )
    rank = basis.shape[1]
    r, place = iota((rank, rank), 0), iota((rank, rank), 1)
    for which in range(CORE):
        side = core if which == 0 else 1 - core
        for half in range(2):
            move = one_hot((r == rank_of(place, side)) & (((place >> 2) & 1) == half))
            out_ref[2 * which + half] = jnp.dot(
                basis, move, preferred_element_type=F32
            ).astype(BF16)


def expand_own(basis_ref, directions_ref, out_ref):
    width = directions_ref.shape[1]
    tile = 256
    for half in range(2):
        basis = basis_ref[half]
        for start in range(0, width, tile):
            out_ref[:, half * width + start : half * width + start + tile] = jnp.dot(
                basis, directions_ref[:, start : start + tile], preferred_element_type=F32
            )


def expand(basis_ref, part_ref, directions_ref, out_ref):
    width = directions_ref.shape[1]
    tile = 256
    for half in range(2):
        basis = basis_ref[2 + half]
        for start in range(0, width, tile):
            columns = slice(half * width + start, half * width + start + tile)
            out_ref[:, columns] = (
                part_ref[:, columns]
                + jnp.dot(
                    basis, directions_ref[:, start : start + tile], preferred_element_type=F32
                )
            ).astype(BF16)


def per_device(tokens, grad_gate, basis, first_moment, second_moment):
    rows, features = tokens.shape
    own, rank = basis.shape
    group_tokens, columns = grad_gate.shape
    half = columns // 2
    scale = 1.0 / math.sqrt(group_tokens * Z * Y_LO * CORE)
    shape = jax.ShapeDtypeStruct
    swap = [(0, 1), (1, 0)]

    def exchange(array, axes):
        return lax.all_to_all(array, axes, 0, 0, tiled=True)

    copies = Z * Y_LO * Y_HI
    basis_copies = jnp.broadcast_to(basis[None], (copies, own, rank))
    class_basis = exchange(basis_copies, ("z", "y_lo", "y_hi")).reshape(copies * own, rank)
    block = shape((rows, features // X), BF16)
    blocks = call(split_features, (block,) * X, 2 * rows * features * 512, 0)(tokens)
    arrived = {
        step: lax.ppermute(blocks[step], "x", [(x, (x + step) % X) for x in range(X)])
        for step in (2, 1, 3)
    }
    held = [blocks[0]] + [arrived[step] for step in range(1, X)]
    stacked = call(
        stack, shape((X * rows, features // X), BF16), rows * features, 4 * rows * features
    )(*held)
    class_basis, stacked = lax.optimization_barrier((class_basis, stacked))
    sibling_basis = lax.ppermute(class_basis, "core", swap)
    part_shape = shape((X, rows, rank), F32)
    part_cost = (rows * features * rank, rows * features + copies * own * rank)
    part = call(partial_coefficients, part_shape, *part_cost)(class_basis, stacked)
    parts = call(whole_coefficients, part_shape, *part_cost)(
        sibling_basis, part, stacked
    )
    parts = exchange(parts, "x")
    takers = Y_HI * X
    chunk = rows + own
    gathered = exchange(
        call(
            sum_coefficients,
            shape((takers, chunk, rank), BF16),
            X * rows * rank,
            4 * takers * chunk * rank,
        )(parts, basis),
        ("y_hi", "x"),
    ).reshape(takers * chunk, rank)

    def projected(own_half, dtype):
        return call(
            functools.partial(project, scale, own_half),
            shape((rank, half), dtype),
            2 * rank * group_tokens * columns,
            2 * group_tokens * columns + 2 * rank * columns,
            )(gathered, grad_gate)

    theirs = lax.ppermute(projected(False, BF16), "core", swap)
    mine = projected(True, F32)
    pair = call(add_halves, shape((rank, half), BF16), rank * half, 8 * rank * half)(mine, theirs)
    owned = exchange(pair, ("z", "y_lo"))
    first_out, second_out, direction = call(
        adam,
        (
            shape(first_moment.shape, F32),
            shape(second_moment.shape, F32),
            shape((rank, half), BF16),
        ),
        rank * half,
        4 * rank * half,
    )(owned, first_moment, second_moment)
    directions = exchange(direction, ("z", "y_lo"))
    others = lax.ppermute(directions, "core", swap)
    update_rows = own * takers
    bases = call(
        arrange_basis, shape((4, update_rows, rank), BF16), 8 * update_rows * rank * rank, 0
    )(gathered)
    cost = (4 * update_rows * rank * half, 4 * update_rows * columns)
    part = call(expand_own, shape((update_rows, columns), F32), *cost)(bases, directions)
    update = call(expand, shape((update_rows, columns), BF16), *cost)(bases, part, others)
    return (update, first_out, second_out)


def solution(mesh):
    names = ("z", "y_lo", "core", "y_hi", "x")
    fine = Mesh(mesh.devices.reshape(Z, Y_LO, CORE, Y_HI, X), names)
    data, tensor = names[:3], names[3:]
    placed = (P(names, None), P(data, tensor), P(names, None), P(data, tensor), P(data, tensor))
    return jax.shard_map(
        per_device,
        mesh=fine,
        in_specs=placed,
        out_specs=(P(data, tensor), P(data, tensor), P(data, tensor)),
        check_vma=False,
    )
```
